256 devices in a mesh: dp: 4 (over y), ty: 4 (over z_hi, core), tx: 16 (over z_lo, x).
Axes of the slice: x: 4, y: 4, z: 8 (z_hi: 2, z_lo: 4; z = z_hi * 4 + z_lo), core: 2. Of those that a mesh axis runs over, the one named last changes fastest.
Arguments:
- features: bfloat16 [4, 256, 1024, 128], P('dp', 'ty', 'tx'), may hold values from -6 to 6
- filter_one: bfloat16 [3, 3, 128, 128], P(None, None, None, 'dp'), may hold values from -0.1875 to 0.1875
- filter_two: bfloat16 [3, 3, 128, 128], P(None, None, None, 'dp'), may hold values from -0.1875 to 0.1875
- speedup: float32 [4, 256, 1024], P('dp', 'ty', 'tx'), may hold values from 0.5 to 2
- land_mask: int32 [4, 256, 1024], P('dp', 'ty', 'tx'), may hold values 0 or 1
- offsets: int32 [4, 2], P('dp'), may hold values from 0 to 1023
- upstream: bfloat16 [4, 256, 1024, 128], P('dp', 'ty', 'tx'), may hold values from -6 to 6
Outputs:
- output: bfloat16 [4, 256, 1024, 128], P('dp', 'ty', 'tx')
- grad_input: bfloat16 [4, 256, 1024, 128], P('dp', 'ty', 'tx')
- grad_one: float32 [3, 3, 128, 128], P(None, None, None, 'dp')
- grad_two: float32 [3, 3, 128, 128], P(None, None, None, 'dp')
The draws below stay inside these ranges and needn't reach their ends.
All inputs are finite; a program needn't handle non-finite values. No bound on the sum of `land_mask` on one device may be relied on, other than what follows from the above.
Results may differ from the reference program's by a relative error of at most 0.014.
Values may be sent and summed in bfloat16 or wider, within the bound.
A program may use at most 64 MiB of HBM per device.

```python
import math
import jax
import jax.numpy as jnp
from jax import lax

C = 128
BATCH = 4
CROP_H = 256
CROP_W = 1024


def place_ends(result, key, smallest, largest):
    longest = result.shape.index(max(result.shape))
    spots = []
    for shift in (0, 1):
        where = [jax.random.randint(jax.random.fold_in(key, axis), (), 0, length) for axis, length in enumerate(result.shape)]
        where[longest] = (where[longest] + shift) % result.shape[longest]
        spots.append(tuple(where))
    return result.at[spots[0]].set(smallest).at[spots[1]].set(largest)


def with_spikes(values, rng, source, target, shards_of, factor):
    owner, partner = [(jnp.arange(values.shape[position]) // (values.shape[position] // shards_of)).reshape([-1 if axis == position else 1 for axis in range(values.ndim)]) for position in (source, target)]
    chosen = jax.random.permutation(rng, shards_of)[partner]
    strong = (owner == chosen) | (owner == (partner + shards_of // 2) % shards_of)
    return jnp.where(strong, factor * values, values)


def steps_of(stream_key, dims, cuts, low, high):
    loudness, own = 1.0, jax.random.fold_in(stream_key, 6)
    for axis_at, parts in cuts:
        draws = jnp.exp(jax.random.uniform(jax.random.fold_in(own, axis_at), (parts,), jnp.float32, low / len(cuts), high / len(cuts)))
        loudness = loudness * jnp.repeat(draws, dims[axis_at] // parts).reshape([-1 if axis == axis_at else 1 for axis in range(len(dims))])
    return loudness


def gaussian(own_key, shape, deviation, most, cuts=(), kind=jnp.bfloat16):
    values = jax.random.normal(own_key, shape, jnp.float32) * deviation
    if len(cuts) > 0:
        values = steps_of(own_key, shape, cuts, -0.22, 0.18) * values
    return jnp.clip(values, min=-most, max=most).astype(kind)


def heavy_noise(rng, shape, deviation, most, split, heavy, kind=jnp.bfloat16):
    values = deviation * jax.random.normal(rng, shape, jnp.float32)
    if split:
        values = values * steps_of(rng, shape, split, -0.22, 0.18)
    return jnp.clip(with_spikes(values, jax.random.fold_in(rng, 3), *heavy), -most, most).astype(kind)


def setup_inputs(seed: int = 0) -> dict:
    streams_of = jax.random.split(jax.random.key(seed), 8)
    return {
        "features": gaussian(streams_of[0], (BATCH, CROP_H, CROP_W, C), 1.0, 6.0, ((0, 4), (1, 4), (2, 16))),
        "filter_one": gaussian(streams_of[1], (3, 3, C, C), (9 * C) ** -0.5, 0.1875, ((3, 4),)),
        "filter_two": gaussian(streams_of[2], (3, 3, C, C), (9 * C) ** -0.5, 0.1875, ((3, 4),)),
        "speedup": jnp.clip(jnp.exp(math.log(2.0) - 1.3862944 * jax.random.uniform(streams_of[3], (BATCH, CROP_H, CROP_W), jnp.float32) ** steps_of(streams_of[3], (BATCH, CROP_H, CROP_W), ((0, 4), (1, 4), (2, 16)), -0.2, 0.2)), 0.5, 2.0),
        "land_mask": place_ends((jax.random.randint(streams_of[4], (BATCH, CROP_H, CROP_W), 0, 2) < 1).astype(jnp.int32), jax.random.fold_in(streams_of[4], 1), 0, 1),
        "offsets": place_ends(jax.random.randint(streams_of[5], (BATCH, 2), 0, 1024), jax.random.fold_in(streams_of[5], 1), 0, 1023).astype(jnp.int32),
        "upstream": heavy_noise(streams_of[6], (BATCH, CROP_H, CROP_W, C), 1.0, 6.0, ((0, 4), (1, 4), (2, 16)), (0, 3, 4, 2.0)),
    }


def conv_same(values, kernel):
    return lax.conv_general_dilated(values, kernel, (1, 1), ((1, 1), (1, 1)), dimension_numbers=('NHWC', 'HWIO', 'NHWC'), preferred_element_type=jnp.float32)

def flipped(kernel):
    return jnp.flip(kernel, (0, 1)).transpose(0, 1, 3, 2)

def filter_grad(values, grads):
    padded = jnp.pad(values, ((0, 0), (1, 1), (1, 1), (0, 0))).astype(jnp.float32)
    grads32 = grads.astype(jnp.float32)
    height = grads.shape[1]
    breadth = grads.shape[2]
    result_rows = []
    for row_tap in range(3):
        taps_row = []
        for col_tap in range(3):
            window = padded[:, row_tap:row_tap + height, col_tap:col_tap + breadth, :]
            taps_row.append(jnp.einsum('bhwc,bhwd->cd', window, grads32))
        result_rows.append(jnp.stack(taps_row))
    return jnp.stack(result_rows)

def reference(features, filter_one, filter_two, speedup, land_mask, offsets, upstream):
    row_pos = (offsets[:, 0:1] + jnp.arange(CROP_H, dtype=jnp.int32)[None, :]).astype(jnp.float32)
    col_pos = (offsets[:, 1:2] + jnp.arange(CROP_W, dtype=jnp.int32)[None, :]).astype(jnp.float32)
    factor = jnp.where(land_mask == 1, speedup, jnp.float32(1.0))
    factor = factor / (1.0 + row_pos / 512.0)[:, :, None] / (1.0 + col_pos / 1024.0)[:, None, :]
    pre_one = conv_same(features, filter_one)
    sigmoid_one = jax.nn.sigmoid(pre_one)
    hidden = (pre_one * sigmoid_one * factor[..., None]).astype(jnp.bfloat16)
    output = conv_same(hidden, filter_two).astype(jnp.bfloat16)
    grad_hidden = conv_same(upstream, flipped(filter_two))
    grad_pre = (grad_hidden * factor[..., None] * sigmoid_one * (1.0 + pre_one * (1.0 - sigmoid_one))).astype(jnp.bfloat16)
    grad_input = conv_same(grad_pre, flipped(filter_one)).astype(jnp.bfloat16)
    grad_scale = 1.0 / jnp.sqrt(jnp.float32(BATCH * CROP_H * CROP_W))
    grad_two = filter_grad(hidden, upstream) * grad_scale
    grad_one = filter_grad(features, grad_pre) * grad_scale
    return (output, grad_input, grad_one, grad_two)
```

```python
import functools
import math

import jax
import jax.numpy as jnp
from jax import lax
from jax.experimental import pallas as pl
from jax.experimental.pallas import tpu as pltpu
from jax.sharding import PartitionSpec as P

MESH = pl.DeviceIdType.MESH
F32 = jnp.float32
BF16 = jnp.bfloat16

C = 128
T = 64
W = 80
PAIRS = 33
K = 6 * C
TAPS = 9 * C

DIRS = [(-1, -1), (-1, 0), (-1, 1), (0, -1), (0, 1), (1, -1), (1, 0), (1, 1)]


def dot(a, b):
    return jnp.dot(a, b, preferred_element_type=F32)


def kernel(
    sizes, crop, scale,
    features, filter_one, filter_two, speedup, mask, offsets, upstream,
    out, grad_in, grads_t,
    raw, tails, colsend, colrecv, speed_v, mask_v, terrain, factor, filt_v, wt, big,
    x_in, x_up, x_hid, x_gp, up_t, gp_t, pre, gh, rs, gf, gb, p1_recv, pieces_f, pieces_b, p2_recv,
    z_slots, g_full, g_out, out_v,
    local_sem, halo_s, halo_r, terr_s, terr_r, w_s, w_r, p1_s, p1_r, p2_s, p2_r, p4_s, p4_r, p5_s, p5_r, out_sem,
):
    n_dp, n_ty, n_tx = sizes
    n_x = 4
    n_zl = n_tx // n_x
    n_z = (n_ty // 2) * n_zl
    dp, ty, tx = lax.axis_index("dp"), lax.axis_index("ty"), lax.axis_index("tx")
    core, x = lax.rem(ty, 2), lax.rem(tx, n_x)
    zl = tx // n_x
    z = (ty // 2) * n_zl + zl

    def inside(dy, dx):
        ok = None
        if dy:
            ok = (ty > 0) if dy < 0 else (ty < n_ty - 1)
        if dx:
            okx = (tx > 0) if dx < 0 else (tx < n_tx - 1)
            ok = okx if ok is None else jnp.logical_and(ok, okx)
        return ok

    plane = [
        (lax.rem(dp + k // n_x, n_dp), ty, zl * n_x + lax.rem(x + k % n_x, n_x))
        for k in range(1, n_dp * n_x)
    ]

    def z_peer(k):
        to = lax.rem(z + k, n_z)
        return (dp, (to // n_zl) * 2 + core, lax.rem(to, n_zl) * n_x + x)

    z_peers = [z_peer(k) for k in range(1, n_z)]

    def mate(k):
        return (dp, (ty // 2) * 2 + lax.rem(core + k // n_x, 2), zl * n_x + lax.rem(x + k % n_x, n_x))

    mates = [mate(k) for k in range(1, 2 * n_x)]
    partner = mate(n_x)
    dp_peers = [(lax.rem(dp + k, n_dp), ty, tx) for k in range(1, n_dp)]

    def load(src, dst, i):
        copy = pltpu.make_async_copy(src, dst, local_sem.at[i])
        copy.start()
        return copy

    loads = [
        load(filter_one, filt_v.at[0], 0),
        load(filter_two, filt_v.at[1], 1),
        load(features.at[0], raw.at[0, pl.ds(2, T), pl.ds(0, T), :], 2),
        load(upstream.at[0], raw.at[1, pl.ds(2, T), pl.ds(0, T), :], 3),
        load(speedup.at[0], speed_v, 4),
        load(mask.at[0], mask_v, 5),
    ]

    barrier = pltpu.get_barrier_semaphore()
    for peer in plane + z_peers + mates:
        pl.semaphore_signal(barrier, inc=1, device_id=peer, device_id_type=MESH)
    for dy, dx in DIRS:
        @pl.when(inside(dy, dx))
        def _(dy=dy, dx=dx):
            pl.semaphore_signal(barrier, inc=1, device_id=(dp, ty + dy, tx + dx), device_id_type=MESH)
    rows_by = (ty > 0).astype(jnp.int32) + (ty < n_ty - 1).astype(jnp.int32)
    cols_by = (tx > 0).astype(jnp.int32) + (tx < n_tx - 1).astype(jnp.int32)
    awaited = len(plane) + len(z_peers) + len(mates) + rows_by + cols_by + rows_by * cols_by

    own = pl.ds(pl.multiple_of(dp * (C // n_dp), C // n_dp), C // n_dp)
    for f in range(2):
        loads[f].wait()
        for k in range(9):
            wt[f, k, own, :] = filt_v[f, k // 3, k % 3].astype(F32).T.astype(BF16)

    pl.semaphore_wait(barrier, awaited)

    def w_copy(f, k):
        return pltpu.make_async_remote_copy(
            src_ref=wt.at[f, :, own, :], dst_ref=wt.at[f, :, own, :],
            send_sem=w_s.at[f, k], recv_sem=w_r.at[f, k], device_id=dp_peers[k], device_id_type=MESH,
        )

    def w_arrival(f, k):
        rows = C // n_dp
        src = lax.rem(dp - (k + 1) + n_dp, n_dp)
        theirs = pl.ds(pl.multiple_of(src * rows, rows), rows)
        return pltpu.make_async_remote_copy(
            src_ref=wt.at[f, :, theirs, :], dst_ref=wt.at[f, :, theirs, :],
            send_sem=w_s.at[f, k], recv_sem=w_r.at[f, k], device_id=dp_peers[k], device_id_type=MESH,
        )

    for k in range(n_dp - 1):
        w_copy(0, k).start()

    loads[4].wait()
    loads[5].wait()
    local = jnp.where(mask_v[...] == 1, speed_v[...], jnp.float32(1.0))
    terrain[0, pl.ds(8, T), :] = jnp.concatenate([local, jnp.ones((T, C - T), F32)], axis=1)

    def terr_copy(i):
        dy, dx = DIRS[i]
        slot = {0: 0, 1: 1, -1: 2}[dx]
        src = {0: pl.ds(8, T), -1: pl.ds(8, 8), 1: pl.ds(T, 8)}[dy]
        dst = {0: pl.ds(8, T), -1: pl.ds(8 + T, 8), 1: pl.ds(0, 8)}[dy]
        return pltpu.make_async_remote_copy(
            src_ref=terrain.at[0, src, :], dst_ref=terrain.at[slot, dst, :],
            send_sem=terr_s.at[i], recv_sem=terr_r.at[i], device_id=(dp, ty + dy, tx + dx), device_id_type=MESH,
        )

    for i, d in enumerate(DIRS):
        @pl.when(inside(*d))
        def _(i=i):
            terr_copy(i).start()

    for n in range(2):
        loads[2 + n].wait()
        colsend[0, n] = raw[n, pl.ds(2, T), pl.ds(0, 16), :][:, 0:2, :]
        colsend[1, n] = raw[n, pl.ds(2, T), pl.ds(T - 16, 16), :][:, 14:16, :]

    def halo_copy(i):
        dy, dx = DIRS[i]
        if dx == 0:
            src = raw.at[:, pl.ds(2 if dy < 0 else T, 2), pl.ds(0, T), :]
            dst = raw.at[:, pl.ds(T + 2 if dy < 0 else 0, 2), pl.ds(0, T), :]
        else:
            s = {0: pl.ds(0, T), -1: pl.ds(0, 2), 1: pl.ds(T - 2, 2)}[dy]
            t = {0: pl.ds(2, T), -1: pl.ds(T + 2, 2), 1: pl.ds(0, 2)}[dy]
            src = colsend.at[0 if dx < 0 else 1, :, s]
            dst = colrecv.at[1 if dx < 0 else 0, :, t]
        return pltpu.make_async_remote_copy(
            src_ref=src, dst_ref=dst,
            send_sem=halo_s.at[i], recv_sem=halo_r.at[i], device_id=(dp, ty + dy, tx + dx), device_id_type=MESH,
        )

    for i, d in enumerate(DIRS):
        @pl.when(inside(*d))
        def _(i=i):
            halo_copy(i).start()
    for k in range(n_dp - 1):
        w_copy(1, k).start()

    for dy, dx in DIRS:
        @pl.when(jnp.logical_not(inside(dy, dx)))
        def _(dy=dy, dx=dx):
            if dx == 0:
                at = T + 2 if dy > 0 else 0
                raw[:, at:at + 2, 0:T, :] = jnp.zeros((2, 2, T, C), BF16)
            else:
                first, size = {0: (2, T), 1: (T + 2, 2), -1: (0, 2)}[dy]
                colrecv[1 if dx > 0 else 0, :, first:first + size] = jnp.zeros((2, size, 2, C), BF16)
    tails[...] = jnp.zeros_like(tails)

    def transpose_up(m, carry):
        pairs = []
        for u in range(2):
            r = 2 + 4 * m + 2 * u
            pairs.append(jnp.concatenate([raw[1, r, 0:T, :], raw[1, r + 1, 0:T, :]], axis=1))
        block = jnp.concatenate(pairs, axis=0)
        up_t[:, pl.ds(pl.multiple_of(m * C, C), C)] = block.T
        return carry

    lax.fori_loop(0, T // 4, transpose_up, 0)

    for i, d in enumerate(DIRS):
        @pl.when(inside(-d[0], -d[1]))
        def _(i=i):
            terr_copy(i).wait_recv()
    turned = [terrain[s].T for s in range(3)]
    cells = jnp.concatenate([turned[0][0:T], turned[2][0:8], turned[1][T - 8:T]], axis=0)
    lane = lax.broadcasted_iota(jnp.int32, (W, W), 1) - 8
    spot = lax.broadcasted_iota(jnp.int32, (W, W), 0)
    col = jnp.where(spot > T + 8, spot - W, spot)
    row_at, col_at = ty * T + lane, tx * T + col
    live = (row_at >= 0) & (row_at < crop[0]) & (col_at >= 0) & (col_at < crop[1]) & (col <= T) & (col >= -1)
    row_pos = (offsets[0, 0] + row_at).astype(F32)
    col_pos = (offsets[0, 1] + col_at).astype(F32)
    live = live & (lane >= -1) & (lane <= T)
    safe = jnp.where(live, cells, jnp.float32(0.0))
    fac = safe / (1.0 + row_pos / 512.0) / (1.0 + col_pos / 1024.0)
    fac = jnp.where(live, fac, jnp.float32(0.0))
    fac = jnp.concatenate([fac, jnp.zeros((W, C - W), F32)], axis=1)

    def spread(q, rolled):
        for t in range(2):
            factor[q, :, t * C:(t + 1) * C] = jnp.broadcast_to(rolled[:, 7 + t:8 + t], (W, C))
        return pltpu.roll(rolled, C - 2, axis=1)

    lax.fori_loop(0, PAIRS, spread, fac)

    def matrices(i, f, flip):
        for e in range(3):
            big[i, 0, e * C:(e + 1) * C, C:2 * C] = jnp.zeros((C, C), BF16)
            big[i, 1, (3 + e) * C:(4 + e) * C, 0:C] = jnp.zeros((C, C), BF16)
        for a in range(3):
            for e in range(3):
                block = wt[f, 3 * (2 - a) + 2 - e] if flip else wt[f, 3 * a + e].T
                for s in range(2):
                    r = a + s
                    at = (r % 2) * 3 * C + e * C
                    big[i, r // 2, at:at + C, s * C:(s + 1) * C] = block

    for k in range(n_dp - 1):
        w_arrival(0, k).wait_recv()
    matrices(0, 0, False)
    matrices(3, 0, True)

    for i, d in enumerate(DIRS):
        @pl.when(inside(-d[0], -d[1]))
        def _(i=i):
            halo_copy(i).wait_recv()

    for n in range(2):
        tails[n, :, 0:2, :] = colrecv[1, n].astype(F32)
        tails[n, :, 14:16, :] = colrecv[0, n].astype(F32)

    def shifted(q, carry):
        for n, dest in ((0, x_in), (1, x_up)):
            for t in range(2):
                cells = jnp.concatenate([raw[n, 2 * q + t, 0:T, :].astype(F32), tails[n, 2 * q + t]], axis=0)
                for e in range(3):
                    moved = cells if e == 1 else pltpu.roll(cells, 1 if e == 0 else W - 1, axis=0)
                    at = (3 * t + e) * C
                    dest[q, :, at:at + C] = moved.astype(BF16)
        return carry

    lax.fori_loop(0, PAIRS + 1, shifted, 0)
    x_in[PAIRS + 1] = jnp.zeros((W, K), BF16)

    def pair_conv(source, i, first, count, width):
        upper = source[pl.ds(first, count)].reshape(count * width, K)
        lower = source[pl.ds(first + 1, count)].reshape(count * width, K)
        return dot(upper, big[i, 0]) + dot(lower, big[i, 1])

    def conv_one(b, carry):
        pre[pl.ds(11 * b, 11)] = pair_conv(x_in, 0, 11 * b, 11, W).reshape(11, W, 2 * C)
        return carry

    lax.fori_loop(0, 3, conv_one, 0)

    for k in range(n_dp - 1):
        w_arrival(1, k).wait_recv()
    matrices(1, 1, True)
    matrices(2, 1, False)

    def conv_two(b, carry):
        gh[pl.ds(11 * b, 11)] = pair_conv(x_up, 1, 11 * b, 11, W).reshape(11, W, 2 * C)
        return carry

    lax.fori_loop(0, 3, conv_two, 0)

    def pointwise(q, carry):
        for t in range(2):
            lanes = slice(t * C, (t + 1) * C)
            value, fac_q = pre[q, :, lanes], factor[q, :, lanes]
            s = jax.nn.sigmoid(value)
            hid = value * s * fac_q
            gp = gh[q, :, lanes] * fac_q * s * (1.0 + value * (1.0 - s))
            for cells, dest in ((hid, x_hid), (gp, x_gp)):
                for e in range(3):
                    moved = cells if e == 1 else pltpu.roll(cells, 1 if e == 0 else W - 1, axis=0)
                    at = (3 * t + e) * C
                    dest[q, :, at:at + C] = moved[0:T].astype(BF16)
        return carry

    lax.fori_loop(0, PAIRS, pointwise, 0)
    x_gp[PAIRS] = jnp.zeros((T, K), BF16)

    def combine(f):
        half = 3 * C
        parts = (
            rs[0, 0:C, 0:half] + rs[0, C:, half:],
            rs[0, 0:C, half:] + rs[1, C:, 0:half],
            rs[1, 0:C, 0:half] + rs[1, C:, half:],
        )
        for a in range(3):
            part = (parts[a] * scale).reshape(C // 8, 8, half)
            gf[f, :, :, a * half:(a + 1) * half] = part
            gb[f, :, :, a * half:(a + 1) * half] = part.astype(BF16)

    for i in range(2):
        rs[i] = dot(up_t[...], x_hid[i:i + T // 2].reshape(T // 2 * T, K))
    combine(1)

    def transpose_gp(m, carry):
        pairs = []
        for u in range(2):
            q = 2 * m + u
            a = x_gp[q, :, C:2 * C]
            b = x_gp[q, :, 4 * C:5 * C]
            a = jnp.where(q == 0, jnp.zeros_like(a), a)
            b = jnp.where(q == PAIRS - 1, jnp.zeros_like(b), b)
            pairs.append(jnp.concatenate([a, b], axis=1))
        gp_t[:, pl.ds(pl.multiple_of(m * C, C), C)] = jnp.concatenate(pairs, axis=0).T
        return carry

    lax.fori_loop(0, (PAIRS + 1) // 2, transpose_gp, 0)
    for i in range(2):
        cells = x_in[i:i + PAIRS + 1, 0:T, :].reshape((PAIRS + 1) * T, K)
        rs[i] = dot(gp_t[...], cells)
    combine(0)

    p1 = pltpu.make_async_remote_copy(
        src_ref=gb.at[1 - core], dst_ref=p1_recv, send_sem=p1_s, recv_sem=p1_r, device_id=partner, device_id_type=MESH,
    )
    p1.start()

    def rows_out(source, i, dest, slot):
        def block(b, carry):
            y = pair_conv(source, i, 8 * b, 8, T).astype(BF16)
            out_v[slot, pl.ds(8 * b, 8), 0] = y[:, 0:C].reshape(8, T, C)
            out_v[slot, pl.ds(8 * b, 8), 1] = y[:, C:].reshape(8, T, C)
            return carry

        lax.fori_loop(0, 4, block, 0)
        copy = pltpu.make_async_copy(out_v.at[slot], dest, out_sem.at[slot])
        copy.start()
        return copy

    writes = [rows_out(x_hid, 2, out, 0)]

    p1.wait_recv()
    pieces = gf[core] + p1_recv[...].astype(F32)
    pieces_f[...] = pieces
    pieces_b[...] = pieces.astype(BF16)

    def p2_copy(k):
        to_dp, _, to_tx = plane[k]
        return pltpu.make_async_remote_copy(
            src_ref=pieces_b.at[to_dp * n_x + lax.rem(to_tx, n_x)], dst_ref=p2_recv.at[k],
            send_sem=p2_s.at[k], recv_sem=p2_r.at[k], device_id=plane[k], device_id_type=MESH,
        )

    p2 = [p2_copy(k) for k in range(len(plane))]
    for copy in p2:
        copy.start()

    writes.append(rows_out(x_gp, 3, grad_in, 1))

    for copy in p2:
        copy.wait_recv()
    mine = pieces_f[dp * n_x + x]
    for k in range(len(plane)):
        mine = mine + p2_recv[k].astype(F32)

    z_slots[z] = mine.astype(BF16)

    def p4_copy(k, at):
        return pltpu.make_async_remote_copy(
            src_ref=z_slots.at[at], dst_ref=z_slots.at[at],
            send_sem=p4_s.at[k], recv_sem=p4_r.at[k], device_id=z_peers[k], device_id_type=MESH,
        )

    p4 = [p4_copy(k, z) for k in range(len(z_peers))]
    for copy in p4:
        copy.start()
    for k in range(len(z_peers)):
        p4_copy(k, lax.rem(z - (k + 1) + n_z, n_z)).wait_recv()
    total = z_slots[0].astype(F32)
    for k in range(1, n_z):
        total = total + z_slots[k].astype(F32)

    g_full[core, x] = total.astype(BF16)

    def p5_copy(k, at_core, at_x):
        return pltpu.make_async_remote_copy(
            src_ref=g_full.at[at_core, at_x], dst_ref=g_full.at[at_core, at_x],
            send_sem=p5_s.at[k], recv_sem=p5_r.at[k], device_id=mates[k], device_id_type=MESH,
        )

    p5 = [p5_copy(k, core, x) for k in range(len(mates))]
    for copy in p5:
        copy.start()
    for k in range(len(mates)):
        dc, dx = (k + 1) // n_x, (k + 1) % n_x
        p5_copy(k, lax.rem(core + dc, 2), lax.rem(x - dx + n_x, n_x)).wait_recv()
    g_out[...] = g_full[...].astype(F32)
    last = pltpu.make_async_copy(g_out, grads_t, out_sem.at[2])
    last.start()

    for copy in p2 + p4 + p5:
        copy.wait_send()
    p1.wait_send()
    for f in range(2):
        for k in range(n_dp - 1):
            w_copy(f, k).wait_send()
    for i, d in enumerate(DIRS):
        @pl.when(inside(*d))
        def _(i=i):
            terr_copy(i).wait_send()
            halo_copy(i).wait_send()
    for copy in writes:
        copy.wait()
    last.wait()


def on_device(sizes, features, filter_one, filter_two, speedup, land_mask, offsets, upstream):
    n_dp, n_ty, n_tx = sizes
    n_x = 4
    n_z = n_ty * n_tx // (2 * n_x)
    rows = C // (n_dp * n_x)
    crop = (n_ty * T, n_tx * T)
    scale = 1.0 / math.sqrt(n_dp * crop[0] * crop[1])
    anywhere = pl.BlockSpec(memory_space=pl.ANY)
    vmem = pltpu.VMEM
    dma = pltpu.SemaphoreType.DMA
    n_plane, n_mates = n_dp * n_x - 1, 2 * n_x - 1
    scratch = [
        vmem((2, T + 4, W, C), BF16),
        vmem((2, T + 4, 16, C), F32),
        vmem((2, 2, T, 2, C), BF16),
        vmem((2, 2, T + 4, 2, C), BF16),
        vmem((T, T), F32),
        vmem((T, T), jnp.int32),
        vmem((3, W, C), F32),
        vmem((PAIRS, W, 2 * C), F32),
        vmem((2, 3, 3, C, C // n_dp), BF16),
        vmem((2, 9, C, C), BF16),
        vmem((4, 2, K, 2 * C), BF16),
        vmem((PAIRS + 2, W, K), BF16),
        vmem((PAIRS + 1, W, K), BF16),
        vmem((PAIRS, T, K), BF16),
        vmem((PAIRS + 1, T, K), BF16),
        vmem((2 * C, T * T // 2), BF16),
        vmem((2 * C, (PAIRS + 1) * T), BF16),
        vmem((PAIRS, W, 2 * C), F32),
        vmem((PAIRS, W, 2 * C), F32),
        vmem((2, 2 * C, K), F32),
        vmem((2, C // rows, rows, TAPS), F32),
        vmem((2, C // rows, rows, TAPS), BF16),
        vmem((C // rows, rows, TAPS), BF16),
        vmem((C // rows, rows, TAPS), F32),
        vmem((C // rows, rows, TAPS), BF16),
        vmem((n_plane, rows, TAPS), BF16),
        vmem((n_z, rows, TAPS), BF16),
        vmem((2, n_x, rows, TAPS), BF16),
        vmem((2, n_x, rows, TAPS), F32),
        vmem((2, T // 2, 2, T, C), BF16),
        dma((6,)),
        dma((8,)), dma((8,)),
        dma((8,)), dma((8,)),
        dma((2, n_dp - 1)), dma((2, n_dp - 1)),
        dma, dma,
        dma((n_plane,)), dma((n_plane,)),
        dma((n_z - 1,)), dma((n_z - 1,)),
        dma((n_mates,)), dma((n_mates,)),
        dma((3,)),
    ]
    out, grad_in, grads_t = pl.pallas_call(
        functools.partial(kernel, sizes, crop, scale),
        out_shape=(
            jax.ShapeDtypeStruct((T // 2, 2, T, C), BF16),
            jax.ShapeDtypeStruct((T // 2, 2, T, C), BF16),
            jax.ShapeDtypeStruct((2, n_x, rows, TAPS), F32),
        ),
        in_specs=[anywhere] * 5 + [pl.BlockSpec(memory_space=pltpu.SMEM), anywhere],
        out_specs=(anywhere,) * 3,
        scratch_shapes=scratch,
        compiler_params=pltpu.CompilerParams(
            collective_id=0, has_side_effects=True, vmem_limit_bytes=60 * 1024 * 1024
        ),
    )(features, filter_one, filter_two, speedup, land_mask, offsets, upstream)
    grads = grads_t.reshape(2, C // n_dp, 9, C).transpose(0, 2, 3, 1).reshape(2, 3, 3, C, C // n_dp)
    return out.reshape(1, T, T, C), grad_in.reshape(1, T, T, C), grads[0], grads[1]


def solution(mesh):
    tile = P("dp", "ty", "tx", None)
    filters = P(None, None, None, "dp")
    plane = P("dp", "ty", "tx")
    sizes = (mesh.shape["dp"], mesh.shape["ty"], mesh.shape["tx"])
    return jax.shard_map(
        functools.partial(on_device, sizes),
        mesh=mesh,
        in_specs=(tile, filters, filters, plane, plane, P("dp", None), tile),
        out_specs=(tile, tile, filters, filters),
        check_vma=False,
    )
```

```python
import functools
import math

import jax
import jax.numpy as jnp
from jax import lax
from jax.experimental import pallas as pl
from jax.experimental.pallas import tpu as pltpu
from jax.sharding import PartitionSpec as P

MESH = pl.DeviceIdType.MESH
F32 = jnp.float32
BF16 = jnp.bfloat16

C = 128
T = 64
W = 80
PAIRS = 33
K = 6 * C
TAPS = 9 * C

DIRS = [(-1, -1), (-1, 0), (-1, 1), (0, -1), (0, 1), (1, -1), (1, 0), (1, 1)]


def dot(a, b):
    return jnp.dot(a, b, preferred_element_type=F32)


def kernel(
    sizes, crop, scale,
    features, filter_one, filter_two, speedup, mask, offsets, upstream,
    out, grad_in, grad_one, grad_two,
    raw, tails, colsend, colrecv, speed_v, mask_v, off_v, terrain, factor, wt, big,
    x_in, x_up, x_hid, x_gp, up_t, gp_t, pre, gh, rs, gf, gb, p1_recv, pieces_f, pieces_b, p2_recv,
    z_slots, g_full, g_out, out_v,
    local_sem, rows_s, rows_r, halo_s, halo_r, terr_s, terr_r, w_s, w_r, p1_s, p1_r, p2_s, p2_r, p4_s, p4_r, p5_s, p5_r, out_sem,
):
    n_dp, n_ty, n_tx = sizes
    n_x = 4
    n_zl = n_tx // n_x
    n_z = (n_ty // 2) * n_zl
    dp, ty, tx = lax.axis_index("dp"), lax.axis_index("ty"), lax.axis_index("tx")
    core, x = lax.rem(ty, 2), lax.rem(tx, n_x)
    zl = tx // n_x
    z = (ty // 2) * n_zl + zl

    def inside(dy, dx):
        ok = None
        if dy:
            ok = (ty > 0) if dy < 0 else (ty < n_ty - 1)
        if dx:
            okx = (tx > 0) if dx < 0 else (tx < n_tx - 1)
            ok = okx if ok is None else jnp.logical_and(ok, okx)
        return ok

    plane = [
        (lax.rem(dp + k // n_x, n_dp), ty, zl * n_x + lax.rem(x + k % n_x, n_x))
        for k in range(1, n_dp * n_x)
    ]

    def z_peer(k):
        to = lax.rem(z + k, n_z)
        return (dp, (to // n_zl) * 2 + core, lax.rem(to, n_zl) * n_x + x)

    z_peers = [z_peer(k) for k in range(1, n_z)]

    def mate(k):
        return (dp, (ty // 2) * 2 + lax.rem(core + k // n_x, 2), zl * n_x + lax.rem(x + k % n_x, n_x))

    mates = [mate(k) for k in range(1, 2 * n_x)]
    partner = mate(n_x)
    dp_peers = [(lax.rem(dp + k, n_dp), ty, tx) for k in range(1, n_dp)]

    def load(src, dst, i):
        copy = pltpu.make_async_copy(src, dst, local_sem.at[i])
        copy.start()
        return copy

    rows = C // n_dp
    own = pl.ds(pl.multiple_of(dp * rows, rows), rows)
    filters = (filter_one, filter_two)
    loads = [
        load(features.at[0], raw.at[0, pl.ds(2, T), pl.ds(0, T), :], 0),
        load(upstream.at[0], raw.at[1, pl.ds(2, T), pl.ds(0, T), :], 1),
        load(speedup.at[0], speed_v, 2),
        load(mask.at[0], mask_v, 3),
        load(filter_one, wt.at[0, :, own, :], 4),
        load(filter_two, wt.at[1, :, own, :], 5),
        load(offsets, off_v, 6),
    ]

    barrier = pltpu.get_barrier_semaphore()
    for peer in plane + z_peers + mates:
        pl.semaphore_signal(barrier, inc=1, device_id=peer, device_id_type=MESH)
    for dy, dx in DIRS:
        @pl.when(inside(dy, dx))
        def _(dy=dy, dx=dx):
            pl.semaphore_signal(barrier, inc=1, device_id=(dp, ty + dy, tx + dx), device_id_type=MESH)
    rows_by = (ty > 0).astype(jnp.int32) + (ty < n_ty - 1).astype(jnp.int32)
    cols_by = (tx > 0).astype(jnp.int32) + (tx < n_tx - 1).astype(jnp.int32)
    awaited = len(plane) + len(z_peers) + len(mates) + rows_by + cols_by + rows_by * cols_by

    loads[2].wait()
    loads[3].wait()
    local = jnp.where(mask_v[...] == 1, speed_v[...], jnp.float32(1.0))
    terrain[0, pl.ds(8, T), :] = jnp.concatenate([local, jnp.ones((T, C - T), F32)], axis=1)
    for n in range(2):
        loads[n].wait()
        colsend[0, n] = raw[n, pl.ds(2, T), pl.ds(0, 16), :][:, 0:2, :]
        colsend[1, n] = raw[n, pl.ds(2, T), pl.ds(T - 16, 16), :][:, 14:16, :]

    pl.semaphore_wait(barrier, awaited)

    def w_copy(f, k):
        return pltpu.make_async_remote_copy(
            src_ref=filters[f], dst_ref=wt.at[f, :, own, :],
            send_sem=w_s.at[f, k], recv_sem=w_r.at[f, k], device_id=dp_peers[k], device_id_type=MESH,
        )

    def w_arrival(f, k):
        src = lax.rem(dp - (k + 1) + n_dp, n_dp)
        theirs = pl.ds(pl.multiple_of(src * rows, rows), rows)
        return pltpu.make_async_remote_copy(
            src_ref=filters[f], dst_ref=wt.at[f, :, theirs, :],
            send_sem=w_s.at[f, k], recv_sem=w_r.at[f, k], device_id=dp_peers[k], device_id_type=MESH,
        )

    def rows_copy(i, n):
        dy = DIRS[i][0]
        return pltpu.make_async_remote_copy(
            src_ref=(features, upstream)[n].at[0, pl.ds(0 if dy < 0 else T - 2, 2)],
            dst_ref=raw.at[n, pl.ds(T + 2 if dy < 0 else 0, 2), pl.ds(0, T), :],
            send_sem=rows_s.at[i // 4, n], recv_sem=rows_r.at[i // 4, n],
            device_id=(dp, ty + dy, tx), device_id_type=MESH,
        )

    def halo_copy(i):
        dy, dx = DIRS[i]
        s = {0: pl.ds(0, T), -1: pl.ds(0, 2), 1: pl.ds(T - 2, 2)}[dy]
        t = {0: pl.ds(2, T), -1: pl.ds(T + 2, 2), 1: pl.ds(0, 2)}[dy]
        return pltpu.make_async_remote_copy(
            src_ref=colsend.at[0 if dx < 0 else 1, :, s], dst_ref=colrecv.at[1 if dx < 0 else 0, :, t],
            send_sem=halo_s.at[i], recv_sem=halo_r.at[i], device_id=(dp, ty + dy, tx + dx), device_id_type=MESH,
        )

    def rim_copies(i):
        return [rows_copy(i, n) for n in range(2)] if DIRS[i][1] == 0 else [halo_copy(i)]

    def terr_copy(i):
        dy, dx = DIRS[i]
        slot = {0: 0, 1: 1, -1: 2}[dx]
        src = {0: pl.ds(8, T), -1: pl.ds(8, 8), 1: pl.ds(T, 8)}[dy]
        dst = {0: pl.ds(8, T), -1: pl.ds(8 + T, 8), 1: pl.ds(0, 8)}[dy]
        return pltpu.make_async_remote_copy(
            src_ref=terrain.at[0, src, :], dst_ref=terrain.at[slot, dst, :],
            send_sem=terr_s.at[i], recv_sem=terr_r.at[i], device_id=(dp, ty + dy, tx + dx), device_id_type=MESH,
        )

    beside, above = (3, 4), (0, 1, 2, 5, 6, 7)
    for i in (1, 6) + beside:
        @pl.when(inside(*DIRS[i]))
        def _(i=i):
            for copy in rim_copies(i):
                copy.start()
    for i, d in enumerate(DIRS):
        @pl.when(inside(*d))
        def _(i=i):
            terr_copy(i).start()
    for k in range(n_dp - 1):
        w_copy(0, k).start()
    for i in (0, 2, 5, 7):
        @pl.when(inside(*DIRS[i]))
        def _(i=i):
            halo_copy(i).start()

    for k in range(n_dp - 1):
        w_copy(1, k).start()

    for dy, dx in DIRS:
        @pl.when(jnp.logical_not(inside(dy, dx)))
        def _(dy=dy, dx=dx):
            if dx == 0:
                at = T + 2 if dy > 0 else 0
                raw[:, at:at + 2, 0:T, :] = jnp.zeros((2, 2, T, C), BF16)
            else:
                first, size = {0: (2, T), 1: (T + 2, 2), -1: (0, 2)}[dy]
                colrecv[1 if dx > 0 else 0, :, first:first + size] = jnp.zeros((2, size, 2, C), BF16)
    tails[...] = jnp.zeros_like(tails)

    def transpose_up(m, carry):
        pairs = []
        for u in range(2):
            r = 2 + 4 * m + 2 * u
            pairs.append(jnp.concatenate([raw[1, r, 0:T, :], raw[1, r + 1, 0:T, :]], axis=1))
        block = jnp.concatenate(pairs, axis=0)
        up_t[:, pl.ds(pl.multiple_of(m * C, C), C)] = block.T
        return carry

    lax.fori_loop(0, T // 4, transpose_up, 0)

    def matrices(i, f, flip):
        for e in range(3):
            big[i, 0, e * C:(e + 1) * C, C:2 * C] = jnp.zeros((C, C), BF16)
            big[i, 1, (3 + e) * C:(4 + e) * C, 0:C] = jnp.zeros((C, C), BF16)
        for a in range(3):
            for e in range(3):
                block = wt[f, 3 * (2 - a) + 2 - e] if flip else wt[f, 3 * a + e].T
                for s in range(2):
                    r = a + s
                    at = (r % 2) * 3 * C + e * C
                    big[i, r // 2, at:at + C, s * C:(s + 1) * C] = block

    def await_rim(which):
        for i in which:
            @pl.when(inside(-DIRS[i][0], -DIRS[i][1]))
            def _(i=i):
                for copy in rim_copies(i):
                    copy.wait_recv()

    def shifted(q, carry):
        for n, dest in ((0, x_in), (1, x_up)):
            for t in range(2):
                cells = jnp.concatenate([raw[n, 2 * q + t, 0:T, :].astype(F32), tails[n, 2 * q + t]], axis=0)
                for e in range(3):
                    moved = cells if e == 1 else pltpu.roll(cells, 1 if e == 0 else W - 1, axis=0)
                    at = (3 * t + e) * C
                    dest[q, :, at:at + C] = moved.astype(BF16)
        return carry

    def fill_tails(first, size):
        for n in range(2):
            tails[n, first:first + size, 0:2, :] = colrecv[1, n, first:first + size].astype(F32)
            tails[n, first:first + size, 14:16, :] = colrecv[0, n, first:first + size].astype(F32)

    await_rim(beside)
    fill_tails(2, T)
    lax.fori_loop(1, PAIRS, shifted, 0)
    for i, d in enumerate(DIRS):
        @pl.when(inside(-d[0], -d[1]))
        def _(i=i):
            terr_copy(i).wait_recv()
    turned = [terrain[s].T for s in range(3)]
    cells = jnp.concatenate([turned[0][0:T], turned[2][0:8], turned[1][T - 8:T]], axis=0)
    lane = lax.broadcasted_iota(jnp.int32, (W, W), 1) - 8
    spot = lax.broadcasted_iota(jnp.int32, (W, W), 0)
    col = jnp.where(spot > T + 8, spot - W, spot)
    row_at, col_at = ty * T + lane, tx * T + col
    live = (row_at >= 0) & (row_at < crop[0]) & (col_at >= 0) & (col_at < crop[1]) & (col <= T) & (col >= -1)
    loads[6].wait()
    row_pos = (off_v[0, 0] + row_at).astype(F32)
    col_pos = (off_v[0, 1] + col_at).astype(F32)
    live = live & (lane >= -1) & (lane <= T)
    safe = jnp.where(live, cells, jnp.float32(0.0))
    fac = safe / (1.0 + row_pos / 512.0) / (1.0 + col_pos / 1024.0)
    fac = jnp.where(live, fac, jnp.float32(0.0))
    fac = jnp.concatenate([fac, jnp.zeros((W, C - W), F32)], axis=1)

    for q in range(PAIRS):
        for t in range(2):
            at = 2 * q + 7 + t
            factor[q, :, t * C:(t + 1) * C] = jnp.broadcast_to(fac[:, at:at + 1], (W, C))

    loads[4].wait()
    loads[5].wait()
    for k in range(n_dp - 1):
        w_arrival(0, k).wait_recv()
    matrices(0, 0, False)

    def pair_conv(source, i, first, count, width):
        upper = source[pl.ds(first, count)].reshape(count * width, K)
        lower = source[pl.ds(first + 1, count)].reshape(count * width, K)
        return dot(upper, big[i, 0]) + dot(lower, big[i, 1])

    def main_conv(source, i, dest):
        def block(b, carry):
            first = 10 * b + 1
            dest[pl.ds(first, 10)] = pair_conv(source, i, first, 10, W).reshape(10, W, 2 * C)
            return carry

        lax.fori_loop(0, 3, block, 0)

    ends = (0, PAIRS - 2, PAIRS - 1)

    def end_conv(source, i, dest):
        upper = jnp.concatenate([source[q] for q in ends], axis=0)
        lower = jnp.concatenate([source[q + 1] for q in ends], axis=0)
        both = dot(upper, big[i, 0]) + dot(lower, big[i, 1])
        for k, q in enumerate(ends):
            dest[q] = both[k * W:(k + 1) * W]

    main_conv(x_in, 0, pre)
    for k in range(n_dp - 1):
        w_arrival(1, k).wait_recv()
    matrices(1, 1, True)
    main_conv(x_up, 1, gh)

    await_rim(above)
    fill_tails(0, 2)
    fill_tails(T + 2, 2)
    shifted(0, 0)
    shifted(PAIRS, 0)
    x_in[PAIRS + 1] = jnp.zeros((W, K), BF16)
    end_conv(x_in, 0, pre)
    end_conv(x_up, 1, gh)

    def pointwise(q, carry):
        for t in range(2):
            lanes = slice(t * C, (t + 1) * C)
            value, fac_q = pre[q, :, lanes], factor[q, :, lanes]
            s = jax.nn.sigmoid(value)
            hid = value * s * fac_q
            gp = gh[q, :, lanes] * fac_q * s * (1.0 + value * (1.0 - s))
            for cells, dest in ((hid, x_hid), (gp, x_gp)):
                for e in range(3):
                    moved = cells if e == 1 else pltpu.roll(cells, 1 if e == 0 else W - 1, axis=0)
                    at = (3 * t + e) * C
                    dest[q, :, at:at + C] = moved[0:T].astype(BF16)
        return carry

    lax.fori_loop(0, PAIRS, pointwise, 0)
    x_gp[PAIRS] = jnp.zeros((T, K), BF16)

    def combine(f):
        half = 3 * C
        parts = (
            rs[0, 0:C, 0:half] + rs[0, C:, half:],
            rs[0, 0:C, half:] + rs[1, C:, 0:half],
            rs[1, 0:C, 0:half] + rs[1, C:, half:],
        )
        for a in range(3):
            part = (parts[a] * scale).reshape(C // 8, 8, half)
            gf[f, :, :, a * half:(a + 1) * half] = part
            gb[f, :, :, a * half:(a + 1) * half] = part.astype(BF16)

    p1 = pltpu.make_async_remote_copy(
        src_ref=gb.at[1 - core], dst_ref=p1_recv, send_sem=p1_s, recv_sem=p1_r, device_id=partner, device_id_type=MESH,
    )

    def p2_copy(k):
        to_dp, _, to_tx = plane[k]
        return pltpu.make_async_remote_copy(
            src_ref=pieces_b.at[to_dp * n_x + lax.rem(to_tx, n_x)], dst_ref=p2_recv.at[k],
            send_sem=p2_s.at[k], recv_sem=p2_r.at[k], device_id=plane[k], device_id_type=MESH,
        )

    def p4_copy(k, at):
        return pltpu.make_async_remote_copy(
            src_ref=z_slots.at[at], dst_ref=z_slots.at[at],
            send_sem=p4_s.at[k], recv_sem=p4_r.at[k], device_id=z_peers[k], device_id_type=MESH,
        )

    def p5_copy(k, at_core, at_x):
        return pltpu.make_async_remote_copy(
            src_ref=g_full.at[at_core, at_x], dst_ref=g_full.at[at_core, at_x],
            send_sem=p5_s.at[k], recv_sem=p5_r.at[k], device_id=mates[k], device_id_type=MESH,
        )

    def p2_start():
        p1.wait_recv()
        pieces = gf[core] + p1_recv[...].astype(F32)
        pieces_f[...] = pieces
        pieces_b[...] = pieces.astype(BF16)
        for k in range(len(plane)):
            p2_copy(k).start()

    def p4_start():
        for k in range(len(plane)):
            p2_copy(k).wait_recv()
        mine = pieces_f[dp * n_x + x]
        for k in range(len(plane)):
            mine = mine + p2_recv[k].astype(F32)
        z_slots[z] = mine.astype(BF16)
        for k in range(len(z_peers)):
            p4_copy(k, z).start()

    def p5_start():
        for k in range(len(z_peers)):
            p4_copy(k, lax.rem(z - (k + 1) + n_z, n_z)).wait_recv()
        total = z_slots[0].astype(F32)
        for k in range(1, n_z):
            total = total + z_slots[k].astype(F32)
        g_full[core, x] = total.astype(BF16)
        for k in range(len(mates)):
            p5_copy(k, core, x).start()

    def on_core(which, step):
        @pl.when(core == which)
        def _():
            step()

    for m in range((PAIRS + 1) // 2):
        pairs = []
        for q in (2 * m, 2 * m + 1):
            a, b = x_gp[q, :, C:2 * C], x_gp[q, :, 4 * C:5 * C]
            a = jnp.zeros_like(a) if q == 0 else a
            b = jnp.zeros_like(b) if q == PAIRS - 1 else b
            pairs.append(jnp.concatenate([a, b], axis=1))
        gp_t[:, m * C:(m + 1) * C] = jnp.concatenate(pairs, axis=0).T

    for i in range(2):
        rs[i] = dot(up_t[...], x_hid[i:i + T // 2].reshape(T // 2 * T, K))
    combine(1)
    on_core(0, p1.start)

    for i in range(2):
        if i == 1:
            on_core(1, p2_start)
        cells = x_in[i:i + PAIRS + 1, 0:T, :].reshape((PAIRS + 1) * T, K)
        rs[i] = dot(gp_t[...], cells)
    combine(0)
    on_core(1, p1.start)

    matrices(2, 1, False)
    matrices(3, 0, True)

    def rows_out(source, i, slot, first):
        def block(b, carry):
            y = pair_conv(source, i, 8 * b, 8, T).astype(BF16)
            out_v[slot, pl.ds(8 * b, 8), 0] = y[:, 0:C].reshape(8, T, C)
            out_v[slot, pl.ds(8 * b, 8), 1] = y[:, C:].reshape(8, T, C)
            return carry

        lax.fori_loop(first, first + 2, block, 0)

    on_core(0, p2_start)
    on_core(1, p4_start)
    rows_out(x_hid, 2, 0, 0)
    rows_out(x_hid, 2, 0, 2)
    writes = [pltpu.make_async_copy(out_v.at[0], out, out_sem.at[0])]
    writes[0].start()
    on_core(1, p5_start)
    rows_out(x_gp, 3, 1, 0)
    on_core(0, p4_start)
    rows_out(x_gp, 3, 1, 2)
    writes.append(pltpu.make_async_copy(out_v.at[1], grad_in, out_sem.at[1]))
    writes[1].start()
    on_core(0, p5_start)

    for k in range(len(mates)):
        dc, dx = (k + 1) // n_x, (k + 1) % n_x
        p5_copy(k, lax.rem(core + dc, 2), lax.rem(x - dx + n_x, n_x)).wait_recv()
    piece = C // (n_dp * n_x)
    for f, dest in enumerate((grad_one, grad_two)):
        for part in range(n_x):
            for k in range(9):
                g_out[f, k, part * piece:(part + 1) * piece, :] = g_full[f, part, :, k * C:(k + 1) * C].astype(F32)
        writes.append(pltpu.make_async_copy(g_out.at[f], dest, out_sem.at[2 + f]))
        writes[-1].start()

    for k in range(len(plane)):
        p2_copy(k).wait_send()
    for k in range(len(z_peers)):
        p4_copy(k, z).wait_send()
    for k in range(len(mates)):
        p5_copy(k, core, x).wait_send()
    p1.wait_send()
    for f in range(2):
        for k in range(n_dp - 1):
            w_copy(f, k).wait_send()
    for i, d in enumerate(DIRS):
        @pl.when(inside(*d))
        def _(i=i):
            terr_copy(i).wait_send()
            for copy in rim_copies(i):
                copy.wait_send()
    for copy in writes:
        copy.wait()


def by_output(filters):
    return filters.transpose(0, 1, 3, 2).reshape(9, filters.shape[3], C)


def by_input(grads):
    return grads.reshape(3, 3, grads.shape[1], C).transpose(0, 1, 3, 2)


def placed(*refs):
    sources, dests, held, (in_sem, out_sem) = refs[0:4], refs[4:8], refs[8:12], refs[12:14]
    parts = []
    for source, dest, mid in zip(sources, dests, held):
        count = 4 if source.shape[0] % 4 == 0 else 1
        step = source.shape[0] // count
        parts += [(source, dest, mid, pl.ds(p * step, step)) for p in range(count)]
    reads = [
        pltpu.make_async_copy(source.at[at], mid.at[at], in_sem.at[i]) for i, (source, dest, mid, at) in enumerate(parts)
    ]
    writes = [
        pltpu.make_async_copy(mid.at[at], dest.at[at], out_sem.at[i]) for i, (source, dest, mid, at) in enumerate(parts)
    ]
    for copy in reads:
        copy.start()
    for read, write in zip(reads, writes):
        read.wait()
        write.start()
    for copy in writes:
        copy.wait()


def on_device(sizes, features, filter_one, filter_two, speedup, land_mask, offsets, upstream):
    n_dp, n_ty, n_tx = sizes
    n_x = 4
    n_z = n_ty * n_tx // (2 * n_x)
    rows = C // (n_dp * n_x)
    crop = (n_ty * T, n_tx * T)
    scale = 1.0 / math.sqrt(n_dp * crop[0] * crop[1])
    anywhere = pl.BlockSpec(memory_space=pl.ANY)
    vmem = pltpu.VMEM
    dma = pltpu.SemaphoreType.DMA
    n_plane, n_mates = n_dp * n_x - 1, 2 * n_x - 1
    scratch = [
        vmem((2, T + 4, W, C), BF16),
        vmem((2, T + 4, 16, C), F32),
        vmem((2, 2, T, 2, C), BF16),
        vmem((2, 2, T + 4, 2, C), BF16),
        vmem((T, T), F32),
        vmem((T, T), jnp.int32),
        pltpu.SMEM((1, 2), jnp.int32),
        vmem((3, W, C), F32),
        vmem((PAIRS, W, 2 * C), F32),
        vmem((2, 9, C, C), BF16),
        vmem((4, 2, K, 2 * C), BF16),
        vmem((PAIRS + 2, W, K), BF16),
        vmem((PAIRS + 1, W, K), BF16),
        vmem((PAIRS, T, K), BF16),
        vmem((PAIRS + 1, T, K), BF16),
        vmem((2 * C, T * T // 2), BF16),
        vmem((2 * C, (PAIRS + 1) * T), BF16),
        vmem((PAIRS, W, 2 * C), F32),
        vmem((PAIRS, W, 2 * C), F32),
        vmem((2, 2 * C, K), F32),
        vmem((2, C // rows, rows, TAPS), F32),
        vmem((2, C // rows, rows, TAPS), BF16),
        vmem((C // rows, rows, TAPS), BF16),
        vmem((C // rows, rows, TAPS), F32),
        vmem((C // rows, rows, TAPS), BF16),
        vmem((n_plane, rows, TAPS), BF16),
        vmem((n_z, rows, TAPS), BF16),
        vmem((2, n_x, rows, TAPS), BF16),
        vmem((2, 9, C // n_dp, C), F32),
        vmem((2, T // 2, 2, T, C), BF16),
        dma((7,)),
        dma((2, 2)), dma((2, 2)),
        dma((8,)), dma((8,)),
        dma((8,)), dma((8,)),
        dma((2, n_dp - 1)), dma((2, n_dp - 1)),
        dma, dma,
        dma((n_plane,)), dma((n_plane,)),
        dma((n_z - 1,)), dma((n_z - 1,)),
        dma((n_mates,)), dma((n_mates,)),
        dma((4,)),
    ]
    out, grad_in, grad_one, grad_two = pl.pallas_call(
        functools.partial(kernel, sizes, crop, scale),
        out_shape=(
            jax.ShapeDtypeStruct((T // 2, 2, T, C), BF16),
            jax.ShapeDtypeStruct((T // 2, 2, T, C), BF16),
            jax.ShapeDtypeStruct((9, C // n_dp, C), F32),
            jax.ShapeDtypeStruct((9, C // n_dp, C), F32),
        ),
        in_specs=[anywhere] * 7,
        out_specs=(anywhere,) * 4,
        scratch_shapes=scratch,
        compiler_params=pltpu.CompilerParams(
            collective_id=0, has_side_effects=True, vmem_limit_bytes=60 * 1024 * 1024
        ),
    )(features, by_output(filter_one), by_output(filter_two), speedup, land_mask, offsets, upstream)
    results = (out, grad_in, grad_one, grad_two)
    out, grad_in, grad_one, grad_two = pl.pallas_call(
        placed,
        out_shape=tuple(jax.ShapeDtypeStruct(r.shape, r.dtype) for r in results),
        in_specs=[anywhere] * 4,
        out_specs=(anywhere,) * 4,
        scratch_shapes=[vmem(r.shape, r.dtype) for r in results] + [dma((10,)), dma((10,))],
    )(*results)
    return out.reshape(1, T, T, C), grad_in.reshape(1, T, T, C), by_input(grad_one), by_input(grad_two)


def solution(mesh):
    tile = P("dp", "ty", "tx", None)
    filters = P(None, None, None, "dp")
    plane = P("dp", "ty", "tx")
    sizes = (mesh.shape["dp"], mesh.shape["ty"], mesh.shape["tx"])
    return jax.shard_map(
        functools.partial(on_device, sizes),
        mesh=mesh,
        in_specs=(tile, filters, filters, plane, plane, P("dp", None), tile),
        out_specs=(tile, tile, filters, filters),
        check_vma=False,
    )
```

```python
import functools
import math

import jax
import jax.numpy as jnp
from jax import lax
from jax.experimental import pallas as pl
from jax.experimental.pallas import tpu as pltpu
from jax.sharding import PartitionSpec as P

MESH = pl.DeviceIdType.MESH
F32 = jnp.float32
BF16 = jnp.bfloat16

C = 128
T = 64
W = 80
PAIRS = 33
K = 6 * C
TAPS = 9 * C

DIRS = [(-1, -1), (-1, 0), (-1, 1), (0, -1), (0, 1), (1, -1), (1, 0), (1, 1)]


def dot(a, b):
    return jnp.dot(a, b, preferred_element_type=F32)


def kernel(
    sizes, crop, scale,
    features, filter_one, filter_two, speedup, mask, offsets, upstream,
    out, grad_in, grad_one, grad_two,
    raw, tails, colsend, colrecv, speed_v, mask_v, off_v, terrain, factor, wt, big,
    x_in, x_up, x_hid, x_gp, up_t, gp_t, pre, gh, rs, gf, gb, p1_recv, pieces_f, pieces_b, p2_recv,
    z_slots, g_full,
    local_sem, rows_s, rows_r, halo_s, halo_r, terr_s, terr_r, w_s, w_r, share_s, share_r, p1_s, p1_r, p2_s, p2_r, p4_s, p4_r, p5_s, p5_r,
):
    n_dp, n_ty, n_tx = sizes
    n_x = 4
    n_zl = n_tx // n_x
    n_z = (n_ty // 2) * n_zl
    dp, ty, tx = lax.axis_index("dp"), lax.axis_index("ty"), lax.axis_index("tx")
    core, x = lax.rem(ty, 2), lax.rem(tx, n_x)
    zl = tx // n_x
    z = (ty // 2) * n_zl + zl

    def inside(dy, dx):
        ok = None
        if dy:
            ok = (ty > 0) if dy < 0 else (ty < n_ty - 1)
        if dx:
            okx = (tx > 0) if dx < 0 else (tx < n_tx - 1)
            ok = okx if ok is None else jnp.logical_and(ok, okx)
        return ok

    plane = [
        (lax.rem(dp + k // n_x, n_dp), ty, zl * n_x + lax.rem(x + k % n_x, n_x))
        for k in range(1, n_dp * n_x)
    ]

    def z_peer(k):
        to = lax.rem(z + k, n_z)
        return (dp, (to // n_zl) * 2 + core, lax.rem(to, n_zl) * n_x + x)

    z_peers = [z_peer(k) for k in range(1, n_z)]

    def mate(k):
        return (dp, (ty // 2) * 2 + lax.rem(core + k // n_x, 2), zl * n_x + lax.rem(x + k % n_x, n_x))

    mates = [mate(k) for k in range(1, 2 * n_x)]
    partner = mate(n_x)
    dp_peers = [(lax.rem(dp + k, n_dp), ty, tx) for k in range(1, n_dp)]

    def load(src, dst, i):
        copy = pltpu.make_async_copy(src, dst, local_sem.at[i])
        copy.start()
        return copy

    rows = C // n_dp
    own = pl.ds(pl.multiple_of(dp * rows, rows), rows)
    filters = (filter_one, filter_two)
    loads = [
        load(features.at[0], raw.at[0, pl.ds(2, T), pl.ds(0, T), :], 0),
        load(upstream.at[0], raw.at[1, pl.ds(2, T), pl.ds(0, T), :], 1),
        load(speedup.at[0], speed_v, 2),
        load(mask.at[0], mask_v, 3),
        load(filter_one, wt.at[0, :, own, :], 4),
        load(filter_two, wt.at[1, :, own, :], 5),
        load(offsets, off_v, 6),
    ]

    barrier = pltpu.get_barrier_semaphore()
    for peer in plane + z_peers + mates:
        pl.semaphore_signal(barrier, inc=1, device_id=peer, device_id_type=MESH)
    for dy, dx in DIRS:
        @pl.when(inside(dy, dx))
        def _(dy=dy, dx=dx):
            pl.semaphore_signal(barrier, inc=1, device_id=(dp, ty + dy, tx + dx), device_id_type=MESH)
    rows_by = (ty > 0).astype(jnp.int32) + (ty < n_ty - 1).astype(jnp.int32)
    cols_by = (tx > 0).astype(jnp.int32) + (tx < n_tx - 1).astype(jnp.int32)
    awaited = len(plane) + len(z_peers) + len(mates) + rows_by + cols_by + rows_by * cols_by

    loads[2].wait()
    loads[3].wait()
    local = jnp.where(mask_v[...] == 1, speed_v[...], jnp.float32(1.0))
    terrain[0, pl.ds(8, T), :] = jnp.concatenate([local, jnp.ones((T, C - T), F32)], axis=1)
    for n in range(2):
        loads[n].wait()
        colsend[0, n] = raw[n, pl.ds(2, T), pl.ds(0, 16), :][:, 0:2, :]
        colsend[1, n] = raw[n, pl.ds(2, T), pl.ds(T - 16, 16), :][:, 14:16, :]

    pl.semaphore_wait(barrier, awaited)

    half = rows // 2

    def w_copy(f, k):
        at = pl.ds(pl.multiple_of(core * half, half), half)
        to = pl.ds(pl.multiple_of(dp * rows + core * half, half), half)
        return pltpu.make_async_remote_copy(
            src_ref=filters[f].at[:, at, :], dst_ref=wt.at[f, :, to, :],
            send_sem=w_s.at[f, k], recv_sem=w_r.at[f, k], device_id=dp_peers[k], device_id_type=MESH,
        )

    def from_peer(k, which):
        src = lax.rem(dp - (k + 1) + n_dp, n_dp)
        return pl.ds(pl.multiple_of(src * rows + which * half, half), half)

    def w_arrival(f, k):
        return pltpu.make_async_remote_copy(
            src_ref=filters[f].at[:, pl.ds(0, half), :], dst_ref=wt.at[f, :, from_peer(k, core), :],
            send_sem=w_s.at[f, k], recv_sem=w_r.at[f, k], device_id=dp_peers[k], device_id_type=MESH,
        )

    def w_share(f, k, which):
        at = wt.at[f, :, from_peer(k, which), :]
        return pltpu.make_async_remote_copy(
            src_ref=at, dst_ref=at,
            send_sem=share_s.at[f, k], recv_sem=share_r.at[f, k], device_id=partner, device_id_type=MESH,
        )

    def share_filter(f):
        for k in range(n_dp - 1):
            w_arrival(f, k).wait_recv()
            w_share(f, k, core).start()

    def await_filter(f):
        for k in range(n_dp - 1):
            w_share(f, k, 1 - core).wait_recv()

    def rows_copy(i, n):
        dy = DIRS[i][0]
        return pltpu.make_async_remote_copy(
            src_ref=(features, upstream)[n].at[0, pl.ds(0 if dy < 0 else T - 2, 2)],
            dst_ref=raw.at[n, pl.ds(T + 2 if dy < 0 else 0, 2), pl.ds(0, T), :],
            send_sem=rows_s.at[i // 4, n], recv_sem=rows_r.at[i // 4, n],
            device_id=(dp, ty + dy, tx), device_id_type=MESH,
        )

    def halo_copy(i):
        dy, dx = DIRS[i]
        s = {0: pl.ds(0, T), -1: pl.ds(0, 2), 1: pl.ds(T - 2, 2)}[dy]
        t = {0: pl.ds(2, T), -1: pl.ds(T + 2, 2), 1: pl.ds(0, 2)}[dy]
        return pltpu.make_async_remote_copy(
            src_ref=colsend.at[0 if dx < 0 else 1, :, s], dst_ref=colrecv.at[1 if dx < 0 else 0, :, t],
            send_sem=halo_s.at[i], recv_sem=halo_r.at[i], device_id=(dp, ty + dy, tx + dx), device_id_type=MESH,
        )

    def rim_copies(i):
        return [rows_copy(i, n) for n in range(2)] if DIRS[i][1] == 0 else [halo_copy(i)]

    def terr_copy(i):
        dy, dx = DIRS[i]
        slot = {0: 0, 1: 1, -1: 2}[dx]
        src = {0: pl.ds(8, T), -1: pl.ds(8, 8), 1: pl.ds(T, 8)}[dy]
        dst = {0: pl.ds(8, T), -1: pl.ds(8 + T, 8), 1: pl.ds(0, 8)}[dy]
        return pltpu.make_async_remote_copy(
            src_ref=terrain.at[0, src, :], dst_ref=terrain.at[slot, dst, :],
            send_sem=terr_s.at[i], recv_sem=terr_r.at[i], device_id=(dp, ty + dy, tx + dx), device_id_type=MESH,
        )

    beside, above = (3, 4), (0, 1, 2, 5, 6, 7)
    for k in range(n_dp - 1):
        w_copy(0, k).start()
    for i in beside:
        @pl.when(inside(*DIRS[i]))
        def _(i=i):
            halo_copy(i).start()
    for k in range(n_dp - 1):
        w_copy(1, k).start()
    for i in (1, 6):
        @pl.when(inside(*DIRS[i]))
        def _(i=i):
            for copy in rim_copies(i):
                copy.start()
    for i, d in enumerate(DIRS):
        @pl.when(inside(*d))
        def _(i=i):
            terr_copy(i).start()
    for i in (0, 2, 5, 7):
        @pl.when(inside(*DIRS[i]))
        def _(i=i):
            halo_copy(i).start()


    for dy, dx in DIRS:
        @pl.when(jnp.logical_not(inside(dy, dx)))
        def _(dy=dy, dx=dx):
            if dx == 0:
                at = T + 2 if dy > 0 else 0
                raw[:, at:at + 2, 0:T, :] = jnp.zeros((2, 2, T, C), BF16)
            else:
                first, size = {0: (2, T), 1: (T + 2, 2), -1: (0, 2)}[dy]
                colrecv[1 if dx > 0 else 0, :, first:first + size] = jnp.zeros((2, size, 2, C), BF16)
    tails[...] = jnp.zeros_like(tails)

    def transpose_up(m, carry):
        pairs = []
        for u in range(2):
            r = 2 + 4 * m + 2 * u
            pairs.append(jnp.concatenate([raw[1, r, 0:T, :], raw[1, r + 1, 0:T, :]], axis=1))
        block = jnp.concatenate(pairs, axis=0)
        up_t[:, pl.ds(pl.multiple_of(m * C, C), C)] = block.T
        return carry

    lax.fori_loop(0, T // 4, transpose_up, 0)

    def matrices(i, f, flip):
        for e in range(3):
            big[i, 0, e * C:(e + 1) * C, C:2 * C] = jnp.zeros((C, C), BF16)
            big[i, 1, (3 + e) * C:(4 + e) * C, 0:C] = jnp.zeros((C, C), BF16)
        for a in range(3):
            for e in range(3):
                block = wt[f, 3 * (2 - a) + 2 - e] if flip else wt[f, 3 * a + e].T
                for s in range(2):
                    r = a + s
                    at = (r % 2) * 3 * C + e * C
                    big[i, r // 2, at:at + C, s * C:(s + 1) * C] = block

    def await_rim(which):
        for i in which:
            @pl.when(inside(-DIRS[i][0], -DIRS[i][1]))
            def _(i=i):
                for copy in rim_copies(i):
                    copy.wait_recv()

    def shifted(q, carry):
        for n, dest in ((0, x_in), (1, x_up)):
            for t in range(2):
                cells = jnp.concatenate([raw[n, 2 * q + t, 0:T, :].astype(F32), tails[n, 2 * q + t]], axis=0)
                for e in range(3):
                    moved = cells if e == 1 else pltpu.roll(cells, 1 if e == 0 else W - 1, axis=0)
                    at = (3 * t + e) * C
                    dest[q, :, at:at + C] = moved.astype(BF16)
        return carry

    def fill_tails(first, size):
        for n in range(2):
            tails[n, first:first + size, 0:2, :] = colrecv[1, n, first:first + size].astype(F32)
            tails[n, first:first + size, 14:16, :] = colrecv[0, n, first:first + size].astype(F32)

    await_rim(beside)
    fill_tails(2, T)
    lax.fori_loop(1, PAIRS, shifted, 0)
    share_filter(0)

    for i, d in enumerate(DIRS):
        @pl.when(inside(-d[0], -d[1]))
        def _(i=i):
            terr_copy(i).wait_recv()
    turned = [terrain[s].T for s in range(3)]
    cells = jnp.concatenate([turned[0][0:T], turned[2][0:8], turned[1][T - 8:T]], axis=0)
    lane = lax.broadcasted_iota(jnp.int32, (W, W), 1) - 8
    spot = lax.broadcasted_iota(jnp.int32, (W, W), 0)
    col = jnp.where(spot > T + 8, spot - W, spot)
    row_at, col_at = ty * T + lane, tx * T + col
    live = (row_at >= 0) & (row_at < crop[0]) & (col_at >= 0) & (col_at < crop[1]) & (col <= T) & (col >= -1)
    loads[6].wait()
    row_pos = (off_v[0, 0] + row_at).astype(F32)
    col_pos = (off_v[0, 1] + col_at).astype(F32)
    live = live & (lane >= -1) & (lane <= T)
    safe = jnp.where(live, cells, jnp.float32(0.0))
    fac = safe / (1.0 + row_pos / 512.0) / (1.0 + col_pos / 1024.0)
    fac = jnp.where(live, fac, jnp.float32(0.0))
    fac = jnp.concatenate([fac, jnp.zeros((W, C - W), F32)], axis=1)

    for q in range(PAIRS):
        for t in range(2):
            at = 2 * q + 7 + t
            factor[q, :, t * C:(t + 1) * C] = jnp.broadcast_to(fac[:, at:at + 1], (W, C))

    loads[4].wait()
    loads[5].wait()
    await_filter(0)
    matrices(0, 0, False)
    share_filter(1)

    def pair_conv(source, i, first, count, width):
        upper = source[pl.ds(first, count)].reshape(count * width, K)
        lower = source[pl.ds(first + 1, count)].reshape(count * width, K)
        return dot(upper, big[i, 0]) + dot(lower, big[i, 1])

    def main_conv(source, i, dest):
        def block(b, carry):
            first = 10 * b + 1
            dest[pl.ds(first, 10)] = pair_conv(source, i, first, 10, W).reshape(10, W, 2 * C)
            return carry

        lax.fori_loop(0, 3, block, 0)

    ends = (0, PAIRS - 2, PAIRS - 1)

    def end_conv(source, i, dest):
        upper = jnp.concatenate([source[q] for q in ends], axis=0)
        lower = jnp.concatenate([source[q + 1] for q in ends], axis=0)
        both = dot(upper, big[i, 0]) + dot(lower, big[i, 1])
        for k, q in enumerate(ends):
            dest[q] = both[k * W:(k + 1) * W]

    main_conv(x_in, 0, pre)
    await_filter(1)
    matrices(1, 1, True)
    main_conv(x_up, 1, gh)

    await_rim(above)
    fill_tails(0, 2)
    fill_tails(T + 2, 2)
    shifted(0, 0)
    shifted(PAIRS, 0)
    x_in[PAIRS + 1] = jnp.zeros((W, K), BF16)
    end_conv(x_in, 0, pre)
    end_conv(x_up, 1, gh)

    def pointwise(q, carry):
        for t in range(2):
            lanes = slice(t * C, (t + 1) * C)
            value, fac_q = pre[q, :, lanes], factor[q, :, lanes]
            s = jax.nn.sigmoid(value)
            hid = value * s * fac_q
            gp = gh[q, :, lanes] * fac_q * s * (1.0 + value * (1.0 - s))
            for cells, dest in ((hid, x_hid), (gp, x_gp)):
                for e in range(3):
                    moved = cells if e == 1 else pltpu.roll(cells, 1 if e == 0 else W - 1, axis=0)
                    at = (3 * t + e) * C
                    dest[q, :, at:at + C] = moved[0:T].astype(BF16)
        return carry

    lax.fori_loop(0, PAIRS, pointwise, 0)
    x_gp[PAIRS] = jnp.zeros((T, K), BF16)

    def combine(f):
        half = 3 * C
        parts = (
            rs[0, 0:C, 0:half] + rs[0, C:, half:],
            rs[0, 0:C, half:] + rs[1, C:, 0:half],
            rs[1, 0:C, 0:half] + rs[1, C:, half:],
        )
        for a in range(3):
            part = (parts[a] * scale).reshape(C // 8, 8, half)
            gf[f, :, :, a * half:(a + 1) * half] = part
            gb[f, :, :, a * half:(a + 1) * half] = part.astype(BF16)

    p1 = pltpu.make_async_remote_copy(
        src_ref=gb.at[1 - core], dst_ref=p1_recv, send_sem=p1_s, recv_sem=p1_r, device_id=partner, device_id_type=MESH,
    )

    def p2_copy(k):
        to_dp, _, to_tx = plane[k]
        return pltpu.make_async_remote_copy(
            src_ref=pieces_b.at[to_dp * n_x + lax.rem(to_tx, n_x)], dst_ref=p2_recv.at[k],
            send_sem=p2_s.at[k], recv_sem=p2_r.at[k], device_id=plane[k], device_id_type=MESH,
        )

    def p4_copy(k, at):
        return pltpu.make_async_remote_copy(
            src_ref=z_slots.at[at], dst_ref=z_slots.at[at],
            send_sem=p4_s.at[k], recv_sem=p4_r.at[k], device_id=z_peers[k], device_id_type=MESH,
        )

    def p5_copy(k, at_core, at_x):
        return pltpu.make_async_remote_copy(
            src_ref=g_full.at[at_core, at_x], dst_ref=g_full.at[at_core, at_x],
            send_sem=p5_s.at[k], recv_sem=p5_r.at[k], device_id=mates[k], device_id_type=MESH,
        )

    def p2_start():
        p1.wait_recv()
        pieces = gf[core] + p1_recv[...].astype(F32)
        pieces_f[...] = pieces
        pieces_b[...] = pieces.astype(BF16)
        for k in range(len(plane)):
            p2_copy(k).start()

    def p4_start():
        for k in range(len(plane)):
            p2_copy(k).wait_recv()
        mine = pieces_f[dp * n_x + x]
        for k in range(len(plane)):
            mine = mine + p2_recv[k].astype(F32)
        z_slots[z] = mine.astype(BF16)
        for k in range(len(z_peers)):
            p4_copy(k, z).start()

    def p5_start():
        for k in range(len(z_peers)):
            p4_copy(k, lax.rem(z - (k + 1) + n_z, n_z)).wait_recv()
        total = z_slots[0].astype(F32)
        for k in range(1, n_z):
            total = total + z_slots[k].astype(F32)
        g_full[core, x] = total.astype(BF16)
        for k in range(len(mates)):
            p5_copy(k, core, x).start()

    def on_core(which, step):
        @pl.when(core == which)
        def _():
            step()

    for m in range((PAIRS + 1) // 2):
        pairs = []
        for q in (2 * m, 2 * m + 1):
            a, b = x_gp[q, :, C:2 * C], x_gp[q, :, 4 * C:5 * C]
            a = jnp.zeros_like(a) if q == 0 else a
            b = jnp.zeros_like(b) if q == PAIRS - 1 else b
            pairs.append(jnp.concatenate([a, b], axis=1))
        gp_t[:, m * C:(m + 1) * C] = jnp.concatenate(pairs, axis=0).T

    for i in range(2):
        rs[i] = dot(up_t[...], x_hid[i:i + T // 2].reshape(T // 2 * T, K))
    combine(1)
    on_core(0, p1.start)

    for i in range(2):
        if i == 1:
            on_core(1, p2_start)
        cells = x_in[i:i + PAIRS + 1, 0:T, :].reshape((PAIRS + 1) * T, K)
        rs[i] = dot(gp_t[...], cells)
    combine(0)
    on_core(1, p1.start)

    matrices(2, 1, False)
    matrices(3, 0, True)

    def rows_out(source, i, dest, first):
        def block(b, carry):
            y = pair_conv(source, i, 8 * b, 8, T).astype(BF16)
            dest[pl.ds(8 * b, 8), 0] = y[:, 0:C].reshape(8, T, C)
            dest[pl.ds(8 * b, 8), 1] = y[:, C:].reshape(8, T, C)
            return carry

        lax.fori_loop(first, first + 2, block, 0)

    on_core(0, p2_start)
    on_core(1, p4_start)
    rows_out(x_hid, 2, out, 0)
    rows_out(x_hid, 2, out, 2)
    on_core(1, p5_start)
    rows_out(x_gp, 3, grad_in, 0)
    on_core(0, p4_start)
    rows_out(x_gp, 3, grad_in, 2)
    on_core(0, p5_start)

    for k in range(len(mates)):
        dc, dx = (k + 1) // n_x, (k + 1) % n_x
        p5_copy(k, lax.rem(core + dc, 2), lax.rem(x - dx + n_x, n_x)).wait_recv()
    piece = C // (n_dp * n_x)
    for f, dest in enumerate((grad_one, grad_two)):
        for part in range(n_x):
            for k in range(9):
                dest[k, part * piece:(part + 1) * piece, :] = g_full[f, part, :, k * C:(k + 1) * C].astype(F32)

    for k in range(len(plane)):
        p2_copy(k).wait_send()
    for k in range(len(z_peers)):
        p4_copy(k, z).wait_send()
    for k in range(len(mates)):
        p5_copy(k, core, x).wait_send()
    p1.wait_send()
    for f in range(2):
        for k in range(n_dp - 1):
            w_copy(f, k).wait_send()
            w_share(f, k, core).wait_send()
    for i, d in enumerate(DIRS):
        @pl.when(inside(*d))
        def _(i=i):
            terr_copy(i).wait_send()
            for copy in rim_copies(i):
                copy.wait_send()


def by_output(filters):
    return filters.transpose(0, 1, 3, 2).reshape(9, filters.shape[3], C)


def by_input(grads):
    return grads.reshape(3, 3, grads.shape[1], C).transpose(0, 1, 3, 2)


def placed(*refs):
    sources, dests, sem = refs[0:4], refs[4:8], refs[8]
    copies = [pltpu.make_async_copy(source, dest, sem.at[i]) for i, (source, dest) in enumerate(zip(sources, dests))]
    for copy in copies:
        copy.start()
    for copy in copies:
        copy.wait()


def on_device(sizes, features, filter_one, filter_two, speedup, land_mask, offsets, upstream):
    n_dp, n_ty, n_tx = sizes
    n_x = 4
    n_z = n_ty * n_tx // (2 * n_x)
    rows = C // (n_dp * n_x)
    crop = (n_ty * T, n_tx * T)
    scale = 1.0 / math.sqrt(n_dp * crop[0] * crop[1])
    anywhere = pl.BlockSpec(memory_space=pl.ANY)
    vmem = pltpu.VMEM
    dma = pltpu.SemaphoreType.DMA
    n_plane, n_mates = n_dp * n_x - 1, 2 * n_x - 1
    scratch = [
        vmem((2, T + 4, W, C), BF16),
        vmem((2, T + 4, 16, C), F32),
        vmem((2, 2, T, 2, C), BF16),
        vmem((2, 2, T + 4, 2, C), BF16),
        vmem((T, T), F32),
        vmem((T, T), jnp.int32),
        pltpu.SMEM((1, 2), jnp.int32),
        vmem((3, W, C), F32),
        vmem((PAIRS, W, 2 * C), F32),
        vmem((2, 9, C, C), BF16),
        vmem((4, 2, K, 2 * C), BF16),
        vmem((PAIRS + 2, W, K), BF16),
        vmem((PAIRS + 1, W, K), BF16),
        vmem((PAIRS, T, K), BF16),
        vmem((PAIRS + 1, T, K), BF16),
        vmem((2 * C, T * T // 2), BF16),
        vmem((2 * C, (PAIRS + 1) * T), BF16),
        vmem((PAIRS, W, 2 * C), F32),
        vmem((PAIRS, W, 2 * C), F32),
        vmem((2, 2 * C, K), F32),
        vmem((2, C // rows, rows, TAPS), F32),
        vmem((2, C // rows, rows, TAPS), BF16),
        vmem((C // rows, rows, TAPS), BF16),
        vmem((C // rows, rows, TAPS), F32),
        vmem((C // rows, rows, TAPS), BF16),
        vmem((n_plane, rows, TAPS), BF16),
        vmem((n_z, rows, TAPS), BF16),
        vmem((2, n_x, rows, TAPS), BF16),
        dma((7,)),
        dma((2, 2)), dma((2, 2)),
        dma((8,)), dma((8,)),
        dma((8,)), dma((8,)),
        dma((2, n_dp - 1)), dma((2, n_dp - 1)),
        dma((2, n_dp - 1)), dma((2, n_dp - 1)),
        dma, dma,
        dma((n_plane,)), dma((n_plane,)),
        dma((n_z - 1,)), dma((n_z - 1,)),
        dma((n_mates,)), dma((n_mates,)),
    ]
    out, grad_in, grad_one, grad_two = pl.pallas_call(
        functools.partial(kernel, sizes, crop, scale),
        out_shape=(
            vmem((T // 2, 2, T, C), BF16),
            vmem((T // 2, 2, T, C), BF16),
            vmem((9, C // n_dp, C), F32),
            vmem((9, C // n_dp, C), F32),
        ),
        in_specs=[anywhere] * 7,
        out_specs=(pl.BlockSpec(memory_space=vmem),) * 4,
        scratch_shapes=scratch,
        compiler_params=pltpu.CompilerParams(
            collective_id=0, has_side_effects=True, vmem_limit_bytes=52 * 1024 * 1024
        ),
    )(features, by_output(filter_one), by_output(filter_two), speedup, land_mask, offsets, upstream)
    results = [pltpu.with_memory_space_constraint(r, vmem) for r in (out, grad_in, grad_one, grad_two)]
    out, grad_in, grad_one, grad_two = pl.pallas_call(
        placed,
        out_shape=tuple(jax.ShapeDtypeStruct(r.shape, r.dtype) for r in results),
        in_specs=[pl.BlockSpec(memory_space=vmem)] * 4,
        out_specs=(anywhere,) * 4,
        scratch_shapes=[dma((4,))],
    )(*results)
    return out.reshape(1, T, T, C), grad_in.reshape(1, T, T, C), by_input(grad_one), by_input(grad_two)


def solution(mesh):
    tile = P("dp", "ty", "tx", None)
    filters = P(None, None, None, "dp")
    plane = P("dp", "ty", "tx")
    sizes = (mesh.shape["dp"], mesh.shape["ty"], mesh.shape["tx"])
    return jax.shard_map(
        functools.partial(on_device, sizes),
        mesh=mesh,
        in_specs=(tile, filters, filters, plane, plane, P("dp", None), tile),
        out_specs=(tile, tile, filters, filters),
        check_vma=False,
    )
```

```python
import functools
import math

import jax
import jax.numpy as jnp
from jax import lax
from jax.experimental import pallas as pl
from jax.experimental.pallas import tpu as pltpu
from jax.sharding import PartitionSpec as P

MESH = pl.DeviceIdType.MESH
F32 = jnp.float32
BF16 = jnp.bfloat16

C = 128
T = 64
W = 80
PAIRS = 33
K = 6 * C
TAPS = 9 * C

DIRS = [(-1, -1), (-1, 0), (-1, 1), (0, -1), (0, 1), (1, -1), (1, 0), (1, 1)]


def dot(a, b):
    return jnp.dot(a, b, preferred_element_type=F32)


def kernel(
    sizes, crop, scale,
    features, filter_one, filter_two, speedup, mask, offsets, upstream,
    out, grad_in, grad_one, grad_two,
    raw, tails, colsend, colrecv, speed_v, mask_v, off_v, terrain, factor, wt, big,
    x_in, x_up, x_hid, x_gp, up_t, gp_t, pre, gh, rs, gf, gb, p1_recv, pieces_f, pieces_b, p2_recv,
    z_slots, g_full,
    local_sem, rows_s, rows_r, halo_s, halo_r, terr_s, terr_r, w_s, w_r, share_s, share_r, p1_s, p1_r, p2_s, p2_r, p4_s, p4_r, p5_s, p5_r,
):
    n_dp, n_ty, n_tx = sizes
    n_x = 4
    n_zl = n_tx // n_x
    n_z = (n_ty // 2) * n_zl
    dp, ty, tx = lax.axis_index("dp"), lax.axis_index("ty"), lax.axis_index("tx")
    core, x = lax.rem(ty, 2), lax.rem(tx, n_x)
    zl = tx // n_x
    z = (ty // 2) * n_zl + zl

    def inside(dy, dx):
        ok = None
        if dy:
            ok = (ty > 0) if dy < 0 else (ty < n_ty - 1)
        if dx:
            okx = (tx > 0) if dx < 0 else (tx < n_tx - 1)
            ok = okx if ok is None else jnp.logical_and(ok, okx)
        return ok

    def away(k, n):
        return min(k % n, n - k % n)

    in_plane = sorted(range(1, n_dp * n_x), key=lambda k: -away(k // n_x, n_dp) - away(k, n_x))
    along_z = sorted(range(1, n_z), key=lambda k: -away(k, n_z))
    in_row = sorted(range(1, 2 * n_x), key=lambda k: -2 * away(k, n_x) - k // n_x)

    plane = [
        (lax.rem(dp + k // n_x, n_dp), ty, zl * n_x + lax.rem(x + k % n_x, n_x))
        for k in in_plane
    ]

    def z_peer(k):
        to = lax.rem(z + k, n_z)
        return (dp, (to // n_zl) * 2 + core, lax.rem(to, n_zl) * n_x + x)

    z_peers = [z_peer(k) for k in along_z]

    def mate(k):
        return (dp, (ty // 2) * 2 + lax.rem(core + k // n_x, 2), zl * n_x + lax.rem(x + k % n_x, n_x))

    mates = [mate(k) for k in in_row]
    partner = mate(n_x)
    dp_peers = [(lax.rem(dp + k, n_dp), ty, tx) for k in range(1, n_dp)]

    def load(src, dst, i):
        copy = pltpu.make_async_copy(src, dst, local_sem.at[i])
        copy.start()
        return copy

    rows = C // n_dp
    own = pl.ds(pl.multiple_of(dp * rows, rows), rows)
    filters = (filter_one, filter_two)
    loads = [
        load(features.at[0], raw.at[0, pl.ds(2, T), pl.ds(0, T), :], 0),
        load(upstream.at[0], raw.at[1, pl.ds(2, T), pl.ds(0, T), :], 1),
        load(speedup.at[0], speed_v, 2),
        load(mask.at[0], mask_v, 3),
        load(filter_one, wt.at[0, :, own, :], 4),
        load(filter_two, wt.at[1, :, own, :], 5),
        load(offsets, off_v, 6),
    ]

    barrier = pltpu.get_barrier_semaphore()
    for peer in plane + z_peers + mates:
        pl.semaphore_signal(barrier, inc=1, device_id=peer, device_id_type=MESH)
    for dy, dx in DIRS:
        @pl.when(inside(dy, dx))
        def _(dy=dy, dx=dx):
            pl.semaphore_signal(barrier, inc=1, device_id=(dp, ty + dy, tx + dx), device_id_type=MESH)
    rows_by = (ty > 0).astype(jnp.int32) + (ty < n_ty - 1).astype(jnp.int32)
    cols_by = (tx > 0).astype(jnp.int32) + (tx < n_tx - 1).astype(jnp.int32)
    awaited = len(plane) + len(z_peers) + len(mates) + rows_by + cols_by + rows_by * cols_by

    loads[2].wait()
    loads[3].wait()
    local = jnp.where(mask_v[...] == 1, speed_v[...], jnp.float32(1.0))
    terrain[0, pl.ds(8, T), :] = jnp.concatenate([local, jnp.ones((T, C - T), F32)], axis=1)
    for n in range(2):
        loads[n].wait()
        colsend[0, n] = raw[n, pl.ds(2, T), pl.ds(0, 16), :][:, 0:2, :]
        colsend[1, n] = raw[n, pl.ds(2, T), pl.ds(T - 16, 16), :][:, 14:16, :]

    pl.semaphore_wait(barrier, awaited)

    half = rows // 2

    def w_copy(f, k):
        at = pl.ds(pl.multiple_of(core * half, half), half)
        to = pl.ds(pl.multiple_of(dp * rows + core * half, half), half)
        return pltpu.make_async_remote_copy(
            src_ref=filters[f].at[:, at, :], dst_ref=wt.at[f, :, to, :],
            send_sem=w_s.at[f, k], recv_sem=w_r.at[f, k], device_id=dp_peers[k], device_id_type=MESH,
        )

    def from_peer(k, which):
        src = lax.rem(dp - (k + 1) + n_dp, n_dp)
        return pl.ds(pl.multiple_of(src * rows + which * half, half), half)

    def w_arrival(f, k):
        return pltpu.make_async_remote_copy(
            src_ref=filters[f].at[:, pl.ds(0, half), :], dst_ref=wt.at[f, :, from_peer(k, core), :],
            send_sem=w_s.at[f, k], recv_sem=w_r.at[f, k], device_id=dp_peers[k], device_id_type=MESH,
        )

    def w_share(f, k, which):
        at = wt.at[f, :, from_peer(k, which), :]
        return pltpu.make_async_remote_copy(
            src_ref=at, dst_ref=at,
            send_sem=share_s.at[f, k], recv_sem=share_r.at[f, k], device_id=partner, device_id_type=MESH,
        )

    def share_filter(f):
        for k in range(n_dp - 1):
            w_arrival(f, k).wait_recv()
            w_share(f, k, core).start()

    def await_filter(f):
        for k in range(n_dp - 1):
            w_share(f, k, 1 - core).wait_recv()

    def rows_copy(i, n):
        dy = DIRS[i][0]
        return pltpu.make_async_remote_copy(
            src_ref=(features, upstream)[n].at[0, pl.ds(0 if dy < 0 else T - 2, 2)],
            dst_ref=raw.at[n, pl.ds(T + 2 if dy < 0 else 0, 2), pl.ds(0, T), :],
            send_sem=rows_s.at[i // 4, n], recv_sem=rows_r.at[i // 4, n],
            device_id=(dp, ty + dy, tx), device_id_type=MESH,
        )

    def halo_copy(i):
        dy, dx = DIRS[i]
        s = {0: pl.ds(0, T), -1: pl.ds(0, 2), 1: pl.ds(T - 2, 2)}[dy]
        t = {0: pl.ds(2, T), -1: pl.ds(T + 2, 2), 1: pl.ds(0, 2)}[dy]
        return pltpu.make_async_remote_copy(
            src_ref=colsend.at[0 if dx < 0 else 1, :, s], dst_ref=colrecv.at[1 if dx < 0 else 0, :, t],
            send_sem=halo_s.at[i], recv_sem=halo_r.at[i], device_id=(dp, ty + dy, tx + dx), device_id_type=MESH,
        )

    def rim_copies(i):
        return [rows_copy(i, n) for n in range(2)] if DIRS[i][1] == 0 else [halo_copy(i)]

    def terr_copy(i):
        dy, dx = DIRS[i]
        slot = {0: 0, 1: 1, -1: 2}[dx]
        src = {0: pl.ds(8, T), -1: pl.ds(8, 8), 1: pl.ds(T, 8)}[dy]
        dst = {0: pl.ds(8, T), -1: pl.ds(8 + T, 8), 1: pl.ds(0, 8)}[dy]
        return pltpu.make_async_remote_copy(
            src_ref=terrain.at[0, src, :], dst_ref=terrain.at[slot, dst, :],
            send_sem=terr_s.at[i], recv_sem=terr_r.at[i], device_id=(dp, ty + dy, tx + dx), device_id_type=MESH,
        )

    beside, above = (3, 4), (0, 1, 2, 5, 6, 7)
    for k in range(n_dp - 1):
        w_copy(0, k).start()
    for i in beside:
        @pl.when(inside(*DIRS[i]))
        def _(i=i):
            halo_copy(i).start()
    for k in range(n_dp - 1):
        w_copy(1, k).start()
    for i in (1, 6):
        @pl.when(inside(*DIRS[i]))
        def _(i=i):
            for copy in rim_copies(i):
                copy.start()
    for i, d in enumerate(DIRS):
        @pl.when(inside(*d))
        def _(i=i):
            terr_copy(i).start()
    for i in (0, 2, 5, 7):
        @pl.when(inside(*DIRS[i]))
        def _(i=i):
            halo_copy(i).start()


    for dy, dx in DIRS:
        @pl.when(jnp.logical_not(inside(dy, dx)))
        def _(dy=dy, dx=dx):
            if dx == 0:
                at = T + 2 if dy > 0 else 0
                raw[:, at:at + 2, 0:T, :] = jnp.zeros((2, 2, T, C), BF16)
            else:
                first, size = {0: (2, T), 1: (T + 2, 2), -1: (0, 2)}[dy]
                colrecv[1 if dx > 0 else 0, :, first:first + size] = jnp.zeros((2, size, 2, C), BF16)
    tails[...] = jnp.zeros_like(tails)

    def transpose_up(m, carry):
        pairs = []
        for u in range(2):
            r = 2 + 4 * m + 2 * u
            pairs.append(jnp.concatenate([raw[1, r, 0:T, :], raw[1, r + 1, 0:T, :]], axis=1))
        block = jnp.concatenate(pairs, axis=0)
        up_t[:, pl.ds(pl.multiple_of(m * C, C), C)] = block.T
        return carry

    lax.fori_loop(0, T // 4, transpose_up, 0)

    def matrices(i, f, flip):
        for e in range(3):
            big[i, 0, e * C:(e + 1) * C, C:2 * C] = jnp.zeros((C, C), BF16)
            big[i, 1, (3 + e) * C:(4 + e) * C, 0:C] = jnp.zeros((C, C), BF16)
        for a in range(3):
            for e in range(3):
                block = wt[f, 3 * (2 - a) + 2 - e] if flip else wt[f, 3 * a + e].T
                for s in range(2):
                    r = a + s
                    at = (r % 2) * 3 * C + e * C
                    big[i, r // 2, at:at + C, s * C:(s + 1) * C] = block

    def await_rim(which):
        for i in which:
            @pl.when(inside(-DIRS[i][0], -DIRS[i][1]))
            def _(i=i):
                for copy in rim_copies(i):
                    copy.wait_recv()

    def shifted(q, carry):
        for n, dest in ((0, x_in), (1, x_up)):
            for t in range(2):
                cells = jnp.concatenate([raw[n, 2 * q + t, 0:T, :].astype(F32), tails[n, 2 * q + t]], axis=0)
                for e in range(3):
                    moved = cells if e == 1 else pltpu.roll(cells, 1 if e == 0 else W - 1, axis=0)
                    at = (3 * t + e) * C
                    dest[q, :, at:at + C] = moved.astype(BF16)
        return carry

    def fill_tails(first, size):
        for n in range(2):
            tails[n, first:first + size, 0:2, :] = colrecv[1, n, first:first + size].astype(F32)
            tails[n, first:first + size, 14:16, :] = colrecv[0, n, first:first + size].astype(F32)

    await_rim(beside)
    fill_tails(2, T)
    lax.fori_loop(1, PAIRS, shifted, 0)
    share_filter(0)

    for i, d in enumerate(DIRS):
        @pl.when(inside(-d[0], -d[1]))
        def _(i=i):
            terr_copy(i).wait_recv()
    turned = [terrain[s].T for s in range(3)]
    cells = jnp.concatenate([turned[0][0:T], turned[2][0:8], turned[1][T - 8:T]], axis=0)
    lane = lax.broadcasted_iota(jnp.int32, (W, W), 1) - 8
    spot = lax.broadcasted_iota(jnp.int32, (W, W), 0)
    col = jnp.where(spot > T + 8, spot - W, spot)
    row_at, col_at = ty * T + lane, tx * T + col
    live = (row_at >= 0) & (row_at < crop[0]) & (col_at >= 0) & (col_at < crop[1]) & (col <= T) & (col >= -1)
    loads[6].wait()
    row_pos = (off_v[0, 0] + row_at).astype(F32)
    col_pos = (off_v[0, 1] + col_at).astype(F32)
    live = live & (lane >= -1) & (lane <= T)
    safe = jnp.where(live, cells, jnp.float32(0.0))
    fac = safe / (1.0 + row_pos / 512.0) / (1.0 + col_pos / 1024.0)
    fac = jnp.where(live, fac, jnp.float32(0.0))
    fac = jnp.concatenate([fac, jnp.zeros((W, C - W), F32)], axis=1)

    for q in range(PAIRS):
        for t in range(2):
            at = 2 * q + 7 + t
            factor[q, :, t * C:(t + 1) * C] = jnp.broadcast_to(fac[:, at:at + 1], (W, C))

    loads[4].wait()
    loads[5].wait()
    await_filter(0)
    matrices(0, 0, False)
    share_filter(1)

    def pair_conv(source, i, first, count, width):
        upper = source[pl.ds(first, count)].reshape(count * width, K)
        lower = source[pl.ds(first + 1, count)].reshape(count * width, K)
        return dot(upper, big[i, 0]) + dot(lower, big[i, 1])

    def main_conv(source, i, dest):
        def block(b, carry):
            first = 10 * b + 1
            dest[pl.ds(first, 10)] = pair_conv(source, i, first, 10, W).reshape(10, W, 2 * C)
            return carry

        lax.fori_loop(0, 3, block, 0)

    ends = (0, PAIRS - 2, PAIRS - 1)

    def end_conv(source, i, dest):
        upper = jnp.concatenate([source[q] for q in ends], axis=0)
        lower = jnp.concatenate([source[q + 1] for q in ends], axis=0)
        both = dot(upper, big[i, 0]) + dot(lower, big[i, 1])
        for k, q in enumerate(ends):
            dest[q] = both[k * W:(k + 1) * W]

    main_conv(x_in, 0, pre)
    await_filter(1)
    matrices(1, 1, True)
    main_conv(x_up, 1, gh)

    await_rim(above)
    fill_tails(0, 2)
    fill_tails(T + 2, 2)
    shifted(0, 0)
    shifted(PAIRS, 0)
    x_in[PAIRS + 1] = jnp.zeros((W, K), BF16)
    end_conv(x_in, 0, pre)
    end_conv(x_up, 1, gh)

    def pointwise(q, carry):
        for t in range(2):
            lanes = slice(t * C, (t + 1) * C)
            value, fac_q = pre[q, :, lanes], factor[q, :, lanes]
            s = jax.nn.sigmoid(value)
            hid = value * s * fac_q
            gp = gh[q, :, lanes] * fac_q * s * (1.0 + value * (1.0 - s))
            for cells, dest in ((hid, x_hid), (gp, x_gp)):
                for e in range(3):
                    moved = cells if e == 1 else pltpu.roll(cells, 1 if e == 0 else W - 1, axis=0)
                    at = (3 * t + e) * C
                    dest[q, :, at:at + C] = moved[0:T].astype(BF16)
        return carry

    lax.fori_loop(0, PAIRS, pointwise, 0)
    x_gp[PAIRS] = jnp.zeros((T, K), BF16)

    def combine(f):
        half = 3 * C
        parts = (
            rs[0, 0:C, 0:half] + rs[0, C:, half:],
            rs[0, 0:C, half:] + rs[1, C:, 0:half],
            rs[1, 0:C, 0:half] + rs[1, C:, half:],
        )
        for a in range(3):
            part = (parts[a] * scale).reshape(C // 8, 8, half)
            gf[f, :, :, a * half:(a + 1) * half] = part
            gb[f, :, :, a * half:(a + 1) * half] = part.astype(BF16)

    p1 = pltpu.make_async_remote_copy(
        src_ref=gb.at[1 - core], dst_ref=p1_recv, send_sem=p1_s, recv_sem=p1_r, device_id=partner, device_id_type=MESH,
    )

    def p2_copy(k):
        to_dp, _, to_tx = plane[k]
        return pltpu.make_async_remote_copy(
            src_ref=pieces_b.at[to_dp * n_x + lax.rem(to_tx, n_x)], dst_ref=p2_recv.at[k],
            send_sem=p2_s.at[k], recv_sem=p2_r.at[k], device_id=plane[k], device_id_type=MESH,
        )

    def p4_copy(k, at):
        return pltpu.make_async_remote_copy(
            src_ref=z_slots.at[at], dst_ref=z_slots.at[at],
            send_sem=p4_s.at[k], recv_sem=p4_r.at[k], device_id=z_peers[k], device_id_type=MESH,
        )

    def p5_copy(k, at_core, at_x):
        return pltpu.make_async_remote_copy(
            src_ref=g_full.at[at_core, at_x], dst_ref=g_full.at[at_core, at_x],
            send_sem=p5_s.at[k], recv_sem=p5_r.at[k], device_id=mates[k], device_id_type=MESH,
        )

    def p2_start():
        p1.wait_recv()
        pieces = gf[core] + p1_recv[...].astype(F32)
        pieces_f[...] = pieces
        pieces_b[...] = pieces.astype(BF16)
        for k in range(len(plane)):
            p2_copy(k).start()

    def p4_start():
        for k in range(len(plane)):
            p2_copy(k).wait_recv()
        mine = pieces_f[dp * n_x + x]
        for k in range(len(plane)):
            mine = mine + p2_recv[k].astype(F32)
        z_slots[z] = mine.astype(BF16)
        for k in range(len(z_peers)):
            p4_copy(k, z).start()

    def p5_start():
        for k in range(len(z_peers)):
            p4_copy(k, lax.rem(z - along_z[k] + n_z, n_z)).wait_recv()
        total = z_slots[0].astype(F32)
        for k in range(1, n_z):
            total = total + z_slots[k].astype(F32)
        g_full[core, x] = total.astype(BF16)
        for k in range(len(mates)):
            p5_copy(k, core, x).start()

    def on_core(which, step):
        @pl.when(core == which)
        def _():
            step()

    for m in range((PAIRS + 1) // 2):
        pairs = []
        for q in (2 * m, 2 * m + 1):
            a, b = x_gp[q, :, C:2 * C], x_gp[q, :, 4 * C:5 * C]
            a = jnp.zeros_like(a) if q == 0 else a
            b = jnp.zeros_like(b) if q == PAIRS - 1 else b
            pairs.append(jnp.concatenate([a, b], axis=1))
        gp_t[:, m * C:(m + 1) * C] = jnp.concatenate(pairs, axis=0).T

    for i in range(2):
        rs[i] = dot(up_t[...], x_hid[i:i + T // 2].reshape(T // 2 * T, K))
    combine(1)
    on_core(0, p1.start)

    for i in range(2):
        if i == 1:
            on_core(1, p2_start)
        cells = x_in[i:i + PAIRS + 1, 0:T, :].reshape((PAIRS + 1) * T, K)
        rs[i] = dot(gp_t[...], cells)
    combine(0)
    on_core(1, p1.start)

    matrices(2, 1, False)
    matrices(3, 0, True)

    def rows_out(source, i, dest, first):
        def block(b, carry):
            y = pair_conv(source, i, 8 * b, 8, T).astype(BF16)
            dest[pl.ds(8 * b, 8), 0] = y[:, 0:C].reshape(8, T, C)
            dest[pl.ds(8 * b, 8), 1] = y[:, C:].reshape(8, T, C)
            return carry

        lax.fori_loop(first, first + 2, block, 0)

    on_core(0, p2_start)
    on_core(1, p4_start)
    rows_out(x_hid, 2, out, 0)
    rows_out(x_hid, 2, out, 2)
    on_core(1, p5_start)
    rows_out(x_gp, 3, grad_in, 0)
    on_core(0, p4_start)
    rows_out(x_gp, 3, grad_in, 2)
    on_core(0, p5_start)

    for k in range(len(mates)):
        dc, dx = in_row[k] // n_x, in_row[k] % n_x
        p5_copy(k, lax.rem(core + dc, 2), lax.rem(x - dx + n_x, n_x)).wait_recv()
    piece = C // (n_dp * n_x)
    for f, dest in enumerate((grad_one, grad_two)):
        for part in range(n_x):
            for k in range(9):
                dest[k, part * piece:(part + 1) * piece, :] = g_full[f, part, :, k * C:(k + 1) * C].astype(F32)

    for k in range(len(plane)):
        p2_copy(k).wait_send()
    for k in range(len(z_peers)):
        p4_copy(k, z).wait_send()
    for k in range(len(mates)):
        p5_copy(k, core, x).wait_send()
    p1.wait_send()
    for f in range(2):
        for k in range(n_dp - 1):
            w_copy(f, k).wait_send()
            w_share(f, k, core).wait_send()
    for i, d in enumerate(DIRS):
        @pl.when(inside(*d))
        def _(i=i):
            terr_copy(i).wait_send()
            for copy in rim_copies(i):
                copy.wait_send()


def by_output(filters):
    return filters.transpose(0, 1, 3, 2).reshape(9, filters.shape[3], C)


def by_input(grads):
    return grads.reshape(3, 3, grads.shape[1], C).transpose(0, 1, 3, 2)


def placed(*refs):
    sources, dests, sem = refs[0:4], refs[4:8], refs[8]
    copies = [pltpu.make_async_copy(source, dest, sem.at[i]) for i, (source, dest) in enumerate(zip(sources, dests))]
    for copy in copies:
        copy.start()
    for copy in copies:
        copy.wait()


def on_device(sizes, features, filter_one, filter_two, speedup, land_mask, offsets, upstream):
    n_dp, n_ty, n_tx = sizes
    n_x = 4
    n_z = n_ty * n_tx // (2 * n_x)
    rows = C // (n_dp * n_x)
    crop = (n_ty * T, n_tx * T)
    scale = 1.0 / math.sqrt(n_dp * crop[0] * crop[1])
    anywhere = pl.BlockSpec(memory_space=pl.ANY)
    vmem = pltpu.VMEM
    dma = pltpu.SemaphoreType.DMA
    n_plane, n_mates = n_dp * n_x - 1, 2 * n_x - 1
    scratch = [
        vmem((2, T + 4, W, C), BF16),
        vmem((2, T + 4, 16, C), F32),
        vmem((2, 2, T, 2, C), BF16),
        vmem((2, 2, T + 4, 2, C), BF16),
        vmem((T, T), F32),
        vmem((T, T), jnp.int32),
        pltpu.SMEM((1, 2), jnp.int32),
        vmem((3, W, C), F32),
        vmem((PAIRS, W, 2 * C), F32),
        vmem((2, 9, C, C), BF16),
        vmem((4, 2, K, 2 * C), BF16),
        vmem((PAIRS + 2, W, K), BF16),
        vmem((PAIRS + 1, W, K), BF16),
        vmem((PAIRS, T, K), BF16),
        vmem((PAIRS + 1, T, K), BF16),
        vmem((2 * C, T * T // 2), BF16),
        vmem((2 * C, (PAIRS + 1) * T), BF16),
        vmem((PAIRS, W, 2 * C), F32),
        vmem((PAIRS, W, 2 * C), F32),
        vmem((2, 2 * C, K), F32),
        vmem((2, C // rows, rows, TAPS), F32),
        vmem((2, C // rows, rows, TAPS), BF16),
        vmem((C // rows, rows, TAPS), BF16),
        vmem((C // rows, rows, TAPS), F32),
        vmem((C // rows, rows, TAPS), BF16),
        vmem((n_plane, rows, TAPS), BF16),
        vmem((n_z, rows, TAPS), BF16),
        vmem((2, n_x, rows, TAPS), BF16),
        dma((7,)),
        dma((2, 2)), dma((2, 2)),
        dma((8,)), dma((8,)),
        dma((8,)), dma((8,)),
        dma((2, n_dp - 1)), dma((2, n_dp - 1)),
        dma((2, n_dp - 1)), dma((2, n_dp - 1)),
        dma, dma,
        dma((n_plane,)), dma((n_plane,)),
        dma((n_z - 1,)), dma((n_z - 1,)),
        dma((n_mates,)), dma((n_mates,)),
    ]
    out, grad_in, grad_one, grad_two = pl.pallas_call(
        functools.partial(kernel, sizes, crop, scale),
        out_shape=(
            vmem((T // 2, 2, T, C), BF16),
            vmem((T // 2, 2, T, C), BF16),
            vmem((9, C // n_dp, C), F32),
            vmem((9, C // n_dp, C), F32),
        ),
        in_specs=[anywhere] * 7,
        out_specs=(pl.BlockSpec(memory_space=vmem),) * 4,
        scratch_shapes=scratch,
        compiler_params=pltpu.CompilerParams(
            collective_id=0, has_side_effects=True, vmem_limit_bytes=52 * 1024 * 1024
        ),
    )(features, by_output(filter_one), by_output(filter_two), speedup, land_mask, offsets, upstream)
    results = [pltpu.with_memory_space_constraint(r, vmem) for r in (out, grad_in, grad_one, grad_two)]
    out, grad_in, grad_one, grad_two = pl.pallas_call(
        placed,
        out_shape=tuple(jax.ShapeDtypeStruct(r.shape, r.dtype) for r in results),
        in_specs=[pl.BlockSpec(memory_space=vmem)] * 4,
        out_specs=(anywhere,) * 4,
        scratch_shapes=[dma((4,))],
    )(*results)
    return out.reshape(1, T, T, C), grad_in.reshape(1, T, T, C), by_input(grad_one), by_input(grad_two)


def solution(mesh):
    tile = P("dp", "ty", "tx", None)
    filters = P(None, None, None, "dp")
    plane = P("dp", "ty", "tx")
    sizes = (mesh.shape["dp"], mesh.shape["ty"], mesh.shape["tx"])
    return jax.shard_map(
        functools.partial(on_device, sizes),
        mesh=mesh,
        in_specs=(tile, filters, filters, plane, plane, P("dp", None), tile),
        out_specs=(tile, tile, filters, filters),
        check_vma=False,
    )
```

```python
import functools
import math

import jax
import jax.numpy as jnp
from jax import lax
from jax.experimental import pallas as pl
from jax.experimental.pallas import tpu as pltpu
from jax.sharding import PartitionSpec as P

MESH = pl.DeviceIdType.MESH
F32 = jnp.float32
BF16 = jnp.bfloat16

C = 128
T = 64
W = 80
PAIRS = 33
K = 6 * C
TAPS = 9 * C

DIRS = [(-1, -1), (-1, 0), (-1, 1), (0, -1), (0, 1), (1, -1), (1, 0), (1, 1)]


def dot(a, b):
    return jnp.dot(a, b, preferred_element_type=F32)


def kernel(
    sizes, crop, scale,
    features, filter_one, filter_two, speedup, mask, offsets, upstream,
    out, grad_in, grad_one, grad_two,
    raw, tails, colsend, colrecv, speed_v, mask_v, off_v, terrain, factor, wt, big,
    x_in, x_up, x_hid, x_gp, up_t, gp_t, pre, gh, rs, gf, gb, p1_recv, pieces_f, pieces_b, p2_recv,
    z_slots, g_full,
    local_sem, rows_s, rows_r, halo_s, halo_r, terr_s, terr_r, w_s, w_r, share_s, share_r, p1_s, p1_r, p2_s, p2_r, p4_s, p4_r, p5_s, p5_r,
):
    n_dp, n_ty, n_tx = sizes
    n_x = 4
    n_zl = n_tx // n_x
    n_z = (n_ty // 2) * n_zl
    dp, ty, tx = lax.axis_index("dp"), lax.axis_index("ty"), lax.axis_index("tx")
    core, x = lax.rem(ty, 2), lax.rem(tx, n_x)
    zl = tx // n_x
    z = (ty // 2) * n_zl + zl

    def inside(dy, dx):
        ok = None
        if dy:
            ok = (ty > 0) if dy < 0 else (ty < n_ty - 1)
        if dx:
            okx = (tx > 0) if dx < 0 else (tx < n_tx - 1)
            ok = okx if ok is None else jnp.logical_and(ok, okx)
        return ok

    def away(k, n):
        return min(k % n, n - k % n)

    in_plane = sorted(range(1, n_dp * n_x), key=lambda k: -away(k // n_x, n_dp) - away(k, n_x))
    along_z = sorted(range(1, n_z), key=lambda k: -away(k, n_z))
    in_row = sorted(range(1, 2 * n_x), key=lambda k: -2 * away(k, n_x) - k // n_x)

    plane = [
        (lax.rem(dp + k // n_x, n_dp), ty, zl * n_x + lax.rem(x + k % n_x, n_x))
        for k in in_plane
    ]

    def z_peer(k):
        to = lax.rem(z + k, n_z)
        return (dp, (to // n_zl) * 2 + core, lax.rem(to, n_zl) * n_x + x)

    z_peers = [z_peer(k) for k in along_z]

    def mate(k):
        return (dp, (ty // 2) * 2 + lax.rem(core + k // n_x, 2), zl * n_x + lax.rem(x + k % n_x, n_x))

    mates = [mate(k) for k in in_row]
    partner = mate(n_x)
    dp_peers = [(lax.rem(dp + k, n_dp), ty, tx) for k in range(1, n_dp)]

    def load(src, dst, i):
        copy = pltpu.make_async_copy(src, dst, local_sem.at[i])
        copy.start()
        return copy

    rows = C // n_dp
    own = pl.ds(pl.multiple_of(dp * rows, rows), rows)
    filters = (filter_one, filter_two)
    loads = [
        load(features.at[0], raw.at[0, pl.ds(2, T), pl.ds(0, T), :], 0),
        load(upstream.at[0], raw.at[1, pl.ds(2, T), pl.ds(0, T), :], 1),
        load(speedup.at[0], speed_v, 2),
        load(mask.at[0], mask_v, 3),
        load(filter_one, wt.at[0, :, own, :], 4),
        load(filter_two, wt.at[1, :, own, :], 5),
        load(offsets, off_v, 6),
    ]

    barrier = pltpu.get_barrier_semaphore()
    for peer in plane + z_peers + mates:
        pl.semaphore_signal(barrier, inc=1, device_id=peer, device_id_type=MESH)
    for dy, dx in DIRS:
        @pl.when(inside(dy, dx))
        def _(dy=dy, dx=dx):
            pl.semaphore_signal(barrier, inc=1, device_id=(dp, ty + dy, tx + dx), device_id_type=MESH)
    rows_by = (ty > 0).astype(jnp.int32) + (ty < n_ty - 1).astype(jnp.int32)
    cols_by = (tx > 0).astype(jnp.int32) + (tx < n_tx - 1).astype(jnp.int32)
    awaited = len(plane) + len(z_peers) + len(mates) + rows_by + cols_by + rows_by * cols_by

    loads[2].wait()
    loads[3].wait()
    local = jnp.where(mask_v[...] == 1, speed_v[...], jnp.float32(1.0))
    terrain[0, pl.ds(8, T), :] = jnp.concatenate([local, jnp.ones((T, C - T), F32)], axis=1)
    for n in range(2):
        loads[n].wait()
        colsend[0, n] = raw[n, pl.ds(2, T), pl.ds(0, 16), :][:, 0:2, :]
        colsend[1, n] = raw[n, pl.ds(2, T), pl.ds(T - 16, 16), :][:, 14:16, :]

    pl.semaphore_wait(barrier, awaited)

    half = rows // 2

    def w_copy(f, k):
        at = pl.ds(pl.multiple_of(core * half, half), half)
        to = pl.ds(pl.multiple_of(dp * rows + core * half, half), half)
        return pltpu.make_async_remote_copy(
            src_ref=filters[f].at[:, at, :], dst_ref=wt.at[f, :, to, :],
            send_sem=w_s.at[f, k], recv_sem=w_r.at[f, k], device_id=dp_peers[k], device_id_type=MESH,
        )

    def from_peer(k, which):
        src = lax.rem(dp - (k + 1) + n_dp, n_dp)
        return pl.ds(pl.multiple_of(src * rows + which * half, half), half)

    def w_arrival(f, k):
        return pltpu.make_async_remote_copy(
            src_ref=filters[f].at[:, pl.ds(0, half), :], dst_ref=wt.at[f, :, from_peer(k, core), :],
            send_sem=w_s.at[f, k], recv_sem=w_r.at[f, k], device_id=dp_peers[k], device_id_type=MESH,
        )

    def w_share(f, k, which):
        at = wt.at[f, :, from_peer(k, which), :]
        return pltpu.make_async_remote_copy(
            src_ref=at, dst_ref=at,
            send_sem=share_s.at[f, k], recv_sem=share_r.at[f, k], device_id=partner, device_id_type=MESH,
        )

    def share_filter(f):
        for k in range(n_dp - 1):
            w_arrival(f, k).wait_recv()
            w_share(f, k, core).start()

    def await_filter(f):
        for k in range(n_dp - 1):
            w_share(f, k, 1 - core).wait_recv()

    def rows_copy(i, n):
        dy = DIRS[i][0]
        return pltpu.make_async_remote_copy(
            src_ref=(features, upstream)[n].at[0, pl.ds(0 if dy < 0 else T - 2, 2)],
            dst_ref=raw.at[n, pl.ds(T + 2 if dy < 0 else 0, 2), pl.ds(0, T), :],
            send_sem=rows_s.at[i // 4, n], recv_sem=rows_r.at[i // 4, n],
            device_id=(dp, ty + dy, tx), device_id_type=MESH,
        )

    def halo_copy(i):
        dy, dx = DIRS[i]
        s = {0: pl.ds(0, T), -1: pl.ds(0, 2), 1: pl.ds(T - 2, 2)}[dy]
        t = {0: pl.ds(2, T), -1: pl.ds(T + 2, 2), 1: pl.ds(0, 2)}[dy]
        return pltpu.make_async_remote_copy(
            src_ref=colsend.at[0 if dx < 0 else 1, :, s], dst_ref=colrecv.at[1 if dx < 0 else 0, :, t],
            send_sem=halo_s.at[i], recv_sem=halo_r.at[i], device_id=(dp, ty + dy, tx + dx), device_id_type=MESH,
        )

    def rim_copies(i):
        return [rows_copy(i, n) for n in range(2)] if DIRS[i][1] == 0 else [halo_copy(i)]

    def terr_copy(i):
        dy, dx = DIRS[i]
        slot = {0: 0, 1: 1, -1: 2}[dx]
        src = {0: pl.ds(8, T), -1: pl.ds(8, 8), 1: pl.ds(T, 8)}[dy]
        dst = {0: pl.ds(8, T), -1: pl.ds(8 + T, 8), 1: pl.ds(0, 8)}[dy]
        return pltpu.make_async_remote_copy(
            src_ref=terrain.at[0, src, :], dst_ref=terrain.at[slot, dst, :],
            send_sem=terr_s.at[i], recv_sem=terr_r.at[i], device_id=(dp, ty + dy, tx + dx), device_id_type=MESH,
        )

    beside, above = (3, 4), (0, 1, 2, 5, 6, 7)
    for k in range(n_dp - 1):
        w_copy(0, k).start()
    for i in beside:
        @pl.when(inside(*DIRS[i]))
        def _(i=i):
            halo_copy(i).start()
    for i, d in enumerate(DIRS):
        @pl.when(inside(*d))
        def _(i=i):
            terr_copy(i).start()
    for k in range(n_dp - 1):
        w_copy(1, k).start()
    for i in (1, 6):
        @pl.when(inside(*DIRS[i]))
        def _(i=i):
            for copy in rim_copies(i):
                copy.start()
    for i in (0, 2, 5, 7):
        @pl.when(inside(*DIRS[i]))
        def _(i=i):
            halo_copy(i).start()


    for dy, dx in DIRS:
        @pl.when(jnp.logical_not(inside(dy, dx)))
        def _(dy=dy, dx=dx):
            if dx == 0:
                at = T + 2 if dy > 0 else 0
                raw[:, at:at + 2, 0:T, :] = jnp.zeros((2, 2, T, C), BF16)
            else:
                first, size = {0: (2, T), 1: (T + 2, 2), -1: (0, 2)}[dy]
                colrecv[1 if dx > 0 else 0, :, first:first + size] = jnp.zeros((2, size, 2, C), BF16)
    tails[...] = jnp.zeros_like(tails)

    def transpose_up(m, carry):
        pairs = []
        for u in range(2):
            r = 2 + 4 * m + 2 * u
            pairs.append(jnp.concatenate([raw[1, r, 0:T, :], raw[1, r + 1, 0:T, :]], axis=1))
        block = jnp.concatenate(pairs, axis=0)
        up_t[:, pl.ds(pl.multiple_of(m * C, C), C)] = block.T
        return carry

    lax.fori_loop(0, T // 4, transpose_up, 0)

    def matrices(i, f, flip):
        for e in range(3):
            big[i, 0, e * C:(e + 1) * C, C:2 * C] = jnp.zeros((C, C), BF16)
            big[i, 1, (3 + e) * C:(4 + e) * C, 0:C] = jnp.zeros((C, C), BF16)
        for a in range(3):
            for e in range(3):
                block = wt[f, 3 * (2 - a) + 2 - e] if flip else wt[f, 3 * a + e].T
                for s in range(2):
                    r = a + s
                    at = (r % 2) * 3 * C + e * C
                    big[i, r // 2, at:at + C, s * C:(s + 1) * C] = block

    def await_rim(which):
        for i in which:
            @pl.when(inside(-DIRS[i][0], -DIRS[i][1]))
            def _(i=i):
                for copy in rim_copies(i):
                    copy.wait_recv()

    def shifted(q, carry):
        for n, dest in ((0, x_in), (1, x_up)):
            for t in range(2):
                cells = jnp.concatenate([raw[n, 2 * q + t, 0:T, :].astype(F32), tails[n, 2 * q + t]], axis=0)
                for e in range(3):
                    moved = cells if e == 1 else pltpu.roll(cells, 1 if e == 0 else W - 1, axis=0)
                    at = (3 * t + e) * C
                    dest[q, :, at:at + C] = moved.astype(BF16)
        return carry

    def fill_tails(first, size):
        for n in range(2):
            tails[n, first:first + size, 0:2, :] = colrecv[1, n, first:first + size].astype(F32)
            tails[n, first:first + size, 14:16, :] = colrecv[0, n, first:first + size].astype(F32)

    await_rim(beside)
    fill_tails(2, T)
    lax.fori_loop(1, PAIRS, shifted, 0)
    share_filter(0)

    for i, d in enumerate(DIRS):
        @pl.when(inside(-d[0], -d[1]))
        def _(i=i):
            terr_copy(i).wait_recv()
    turned = [terrain[s].T for s in range(3)]
    cells = jnp.concatenate([turned[0][0:T], turned[2][0:8], turned[1][T - 8:T]], axis=0)
    lane = lax.broadcasted_iota(jnp.int32, (W, W), 1) - 8
    spot = lax.broadcasted_iota(jnp.int32, (W, W), 0)
    col = jnp.where(spot > T + 8, spot - W, spot)
    row_at, col_at = ty * T + lane, tx * T + col
    live = (row_at >= 0) & (row_at < crop[0]) & (col_at >= 0) & (col_at < crop[1]) & (col <= T) & (col >= -1)
    loads[6].wait()
    row_pos = (off_v[0, 0] + row_at).astype(F32)
    col_pos = (off_v[0, 1] + col_at).astype(F32)
    live = live & (lane >= -1) & (lane <= T)
    safe = jnp.where(live, cells, jnp.float32(0.0))
    fac = safe / (1.0 + row_pos / 512.0) / (1.0 + col_pos / 1024.0)
    fac = jnp.where(live, fac, jnp.float32(0.0))
    fac = jnp.concatenate([fac, jnp.zeros((W, C - W), F32)], axis=1)

    for q in range(PAIRS):
        for t in range(2):
            at = 2 * q + 7 + t
            factor[q, :, t * C:(t + 1) * C] = jnp.broadcast_to(fac[:, at:at + 1], (W, C))

    loads[4].wait()
    loads[5].wait()
    await_filter(0)
    matrices(0, 0, False)
    share_filter(1)

    def pair_conv(source, i, first, count, width):
        upper = source[pl.ds(first, count)].reshape(count * width, K)
        lower = source[pl.ds(first + 1, count)].reshape(count * width, K)
        return dot(upper, big[i, 0]) + dot(lower, big[i, 1])

    def main_conv(source, i, dest):
        def block(b, carry):
            first = 10 * b + 1
            dest[pl.ds(first, 10)] = pair_conv(source, i, first, 10, W).reshape(10, W, 2 * C)
            return carry

        lax.fori_loop(0, 3, block, 0)

    ends = (0, PAIRS - 2, PAIRS - 1)

    def end_conv(source, i, dest):
        upper = jnp.concatenate([source[q] for q in ends], axis=0)
        lower = jnp.concatenate([source[q + 1] for q in ends], axis=0)
        both = dot(upper, big[i, 0]) + dot(lower, big[i, 1])
        for k, q in enumerate(ends):
            dest[q] = both[k * W:(k + 1) * W]

    main_conv(x_in, 0, pre)
    await_filter(1)
    matrices(1, 1, True)
    main_conv(x_up, 1, gh)

    await_rim(above)
    fill_tails(0, 2)
    fill_tails(T + 2, 2)
    shifted(0, 0)
    shifted(PAIRS, 0)
    x_in[PAIRS + 1] = jnp.zeros((W, K), BF16)
    end_conv(x_in, 0, pre)
    end_conv(x_up, 1, gh)

    def pointwise(q, carry):
        for t in range(2):
            lanes = slice(t * C, (t + 1) * C)
            value, fac_q = pre[q, :, lanes], factor[q, :, lanes]
            s = jax.nn.sigmoid(value)
            hid = value * s * fac_q
            gp = gh[q, :, lanes] * fac_q * s * (1.0 + value * (1.0 - s))
            for cells, dest in ((hid, x_hid), (gp, x_gp)):
                for e in range(3):
                    moved = cells if e == 1 else pltpu.roll(cells, 1 if e == 0 else W - 1, axis=0)
                    at = (3 * t + e) * C
                    dest[q, :, at:at + C] = moved[0:T].astype(BF16)
        return carry

    lax.fori_loop(0, PAIRS, pointwise, 0)
    x_gp[PAIRS] = jnp.zeros((T, K), BF16)

    def combine(f):
        half = 3 * C
        parts = (
            rs[0, 0:C, 0:half] + rs[0, C:, half:],
            rs[0, 0:C, half:] + rs[1, C:, 0:half],
            rs[1, 0:C, 0:half] + rs[1, C:, half:],
        )
        for a in range(3):
            part = (parts[a] * scale).reshape(C // 8, 8, half)
            gf[f, :, :, a * half:(a + 1) * half] = part
            gb[f, :, :, a * half:(a + 1) * half] = part.astype(BF16)

    p1 = pltpu.make_async_remote_copy(
        src_ref=gb.at[1 - core], dst_ref=p1_recv, send_sem=p1_s, recv_sem=p1_r, device_id=partner, device_id_type=MESH,
    )

    def p2_copy(k):
        to_dp, _, to_tx = plane[k]
        return pltpu.make_async_remote_copy(
            src_ref=pieces_b.at[to_dp * n_x + lax.rem(to_tx, n_x)], dst_ref=p2_recv.at[k],
            send_sem=p2_s.at[k], recv_sem=p2_r.at[k], device_id=plane[k], device_id_type=MESH,
        )

    def p4_copy(k, at):
        return pltpu.make_async_remote_copy(
            src_ref=z_slots.at[at], dst_ref=z_slots.at[at],
            send_sem=p4_s.at[k], recv_sem=p4_r.at[k], device_id=z_peers[k], device_id_type=MESH,
        )

    def p5_copy(k, at_core, at_x):
        return pltpu.make_async_remote_copy(
            src_ref=g_full.at[at_core, at_x], dst_ref=g_full.at[at_core, at_x],
            send_sem=p5_s.at[k], recv_sem=p5_r.at[k], device_id=mates[k], device_id_type=MESH,
        )

    def p2_start():
        p1.wait_recv()
        pieces = gf[core] + p1_recv[...].astype(F32)
        pieces_f[...] = pieces
        pieces_b[...] = pieces.astype(BF16)
        for k in range(len(plane)):
            p2_copy(k).start()

    def p4_start():
        for k in range(len(plane)):
            p2_copy(k).wait_recv()
        mine = pieces_f[dp * n_x + x]
        for k in range(len(plane)):
            mine = mine + p2_recv[k].astype(F32)
        z_slots[z] = mine.astype(BF16)
        for k in range(len(z_peers)):
            p4_copy(k, z).start()

    def p5_start():
        for k in range(len(z_peers)):
            p4_copy(k, lax.rem(z - along_z[k] + n_z, n_z)).wait_recv()
        total = z_slots[0].astype(F32)
        for k in range(1, n_z):
            total = total + z_slots[k].astype(F32)
        g_full[core, x] = total.astype(BF16)
        for k in range(len(mates)):
            p5_copy(k, core, x).start()

    def on_core(which, step):
        @pl.when(core == which)
        def _():
            step()

    for m in range((PAIRS + 1) // 2):
        pairs = []
        for q in (2 * m, 2 * m + 1):
            a, b = x_gp[q, :, C:2 * C], x_gp[q, :, 4 * C:5 * C]
            a = jnp.zeros_like(a) if q == 0 else a
            b = jnp.zeros_like(b) if q == PAIRS - 1 else b
            pairs.append(jnp.concatenate([a, b], axis=1))
        gp_t[:, m * C:(m + 1) * C] = jnp.concatenate(pairs, axis=0).T

    for i in range(2):
        rs[i] = dot(up_t[...], x_hid[i:i + T // 2].reshape(T // 2 * T, K))
    combine(1)
    on_core(0, p1.start)

    for i in range(2):
        if i == 1:
            on_core(1, p2_start)
        cells = x_in[i:i + PAIRS + 1, 0:T, :].reshape((PAIRS + 1) * T, K)
        rs[i] = dot(gp_t[...], cells)
    combine(0)
    on_core(1, p1.start)

    matrices(2, 1, False)
    matrices(3, 0, True)

    def rows_out(source, i, dest, first):
        def block(b, carry):
            y = pair_conv(source, i, 8 * b, 8, T).astype(BF16)
            dest[pl.ds(8 * b, 8), 0] = y[:, 0:C].reshape(8, T, C)
            dest[pl.ds(8 * b, 8), 1] = y[:, C:].reshape(8, T, C)
            return carry

        lax.fori_loop(first, first + 2, block, 0)

    on_core(0, p2_start)
    on_core(1, p4_start)
    rows_out(x_hid, 2, out, 0)
    rows_out(x_hid, 2, out, 2)
    on_core(1, p5_start)
    rows_out(x_gp, 3, grad_in, 0)
    on_core(0, p4_start)
    rows_out(x_gp, 3, grad_in, 2)
    on_core(0, p5_start)

    for k in range(len(mates)):
        dc, dx = in_row[k] // n_x, in_row[k] % n_x
        p5_copy(k, lax.rem(core + dc, 2), lax.rem(x - dx + n_x, n_x)).wait_recv()
    piece = C // (n_dp * n_x)
    for f, dest in enumerate((grad_one, grad_two)):
        for part in range(n_x):
            for k in range(9):
                dest[k, part * piece:(part + 1) * piece, :] = g_full[f, part, :, k * C:(k + 1) * C].astype(F32)

    for k in range(len(plane)):
        p2_copy(k).wait_send()
    for k in range(len(z_peers)):
        p4_copy(k, z).wait_send()
    for k in range(len(mates)):
        p5_copy(k, core, x).wait_send()
    p1.wait_send()
    for f in range(2):
        for k in range(n_dp - 1):
            w_copy(f, k).wait_send()
            w_share(f, k, core).wait_send()
    for i, d in enumerate(DIRS):
        @pl.when(inside(*d))
        def _(i=i):
            terr_copy(i).wait_send()
            for copy in rim_copies(i):
                copy.wait_send()


def by_output(filters):
    return filters.transpose(0, 1, 3, 2).reshape(9, filters.shape[3], C)


def by_input(grads):
    return grads.reshape(3, 3, grads.shape[1], C).transpose(0, 1, 3, 2)


def placed(*refs):
    sources, dests, sem = refs[0:4], refs[4:8], refs[8]
    copies = [pltpu.make_async_copy(source, dest, sem.at[i]) for i, (source, dest) in enumerate(zip(sources, dests))]
    for copy in copies:
        copy.start()
    for copy in copies:
        copy.wait()


def on_device(sizes, features, filter_one, filter_two, speedup, land_mask, offsets, upstream):
    n_dp, n_ty, n_tx = sizes
    n_x = 4
    n_z = n_ty * n_tx // (2 * n_x)
    rows = C // (n_dp * n_x)
    crop = (n_ty * T, n_tx * T)
    scale = 1.0 / math.sqrt(n_dp * crop[0] * crop[1])
    anywhere = pl.BlockSpec(memory_space=pl.ANY)
    vmem = pltpu.VMEM
    dma = pltpu.SemaphoreType.DMA
    n_plane, n_mates = n_dp * n_x - 1, 2 * n_x - 1
    scratch = [
        vmem((2, T + 4, W, C), BF16),
        vmem((2, T + 4, 16, C), F32),
        vmem((2, 2, T, 2, C), BF16),
        vmem((2, 2, T + 4, 2, C), BF16),
        vmem((T, T), F32),
        vmem((T, T), jnp.int32),
        pltpu.SMEM((1, 2), jnp.int32),
        vmem((3, W, C), F32),
        vmem((PAIRS, W, 2 * C), F32),
        vmem((2, 9, C, C), BF16),
        vmem((4, 2, K, 2 * C), BF16),
        vmem((PAIRS + 2, W, K), BF16),
        vmem((PAIRS + 1, W, K), BF16),
        vmem((PAIRS, T, K), BF16),
        vmem((PAIRS + 1, T, K), BF16),
        vmem((2 * C, T * T // 2), BF16),
        vmem((2 * C, (PAIRS + 1) * T), BF16),
        vmem((PAIRS, W, 2 * C), F32),
        vmem((PAIRS, W, 2 * C), F32),
        vmem((2, 2 * C, K), F32),
        vmem((2, C // rows, rows, TAPS), F32),
        vmem((2, C // rows, rows, TAPS), BF16),
        vmem((C // rows, rows, TAPS), BF16),
        vmem((C // rows, rows, TAPS), F32),
        vmem((C // rows, rows, TAPS), BF16),
        vmem((n_plane, rows, TAPS), BF16),
        vmem((n_z, rows, TAPS), BF16),
        vmem((2, n_x, rows, TAPS), BF16),
        dma((7,)),
        dma((2, 2)), dma((2, 2)),
        dma((8,)), dma((8,)),
        dma((8,)), dma((8,)),
        dma((2, n_dp - 1)), dma((2, n_dp - 1)),
        dma((2, n_dp - 1)), dma((2, n_dp - 1)),
        dma, dma,
        dma((n_plane,)), dma((n_plane,)),
        dma((n_z - 1,)), dma((n_z - 1,)),
        dma((n_mates,)), dma((n_mates,)),
    ]
    out, grad_in, grad_one, grad_two = pl.pallas_call(
        functools.partial(kernel, sizes, crop, scale),
        out_shape=(
            vmem((T // 2, 2, T, C), BF16),
            vmem((T // 2, 2, T, C), BF16),
            vmem((9, C // n_dp, C), F32),
            vmem((9, C // n_dp, C), F32),
        ),
        in_specs=[anywhere] * 7,
        out_specs=(pl.BlockSpec(memory_space=vmem),) * 4,
        scratch_shapes=scratch,
        compiler_params=pltpu.CompilerParams(
            collective_id=0, has_side_effects=True, vmem_limit_bytes=52 * 1024 * 1024
        ),
    )(features, by_output(filter_one), by_output(filter_two), speedup, land_mask, offsets, upstream)
    results = [pltpu.with_memory_space_constraint(r, vmem) for r in (out, grad_in, grad_one, grad_two)]
    out, grad_in, grad_one, grad_two = pl.pallas_call(
        placed,
        out_shape=tuple(jax.ShapeDtypeStruct(r.shape, r.dtype) for r in results),
        in_specs=[pl.BlockSpec(memory_space=vmem)] * 4,
        out_specs=(anywhere,) * 4,
        scratch_shapes=[dma((4,))],
    )(*results)
    return out.reshape(1, T, T, C), grad_in.reshape(1, T, T, C), by_input(grad_one), by_input(grad_two)


def solution(mesh):
    tile = P("dp", "ty", "tx", None)
    filters = P(None, None, None, "dp")
    plane = P("dp", "ty", "tx")
    sizes = (mesh.shape["dp"], mesh.shape["ty"], mesh.shape["tx"])
    return jax.shard_map(
        functools.partial(on_device, sizes),
        mesh=mesh,
        in_specs=(tile, filters, filters, plane, plane, P("dp", None), tile),
        out_specs=(tile, tile, filters, filters),
        check_vma=False,
    )
```
